256 devices in a mesh: row: 64 (over z, y, core), rep: 4 (over x).
Axes of the slice: x: 4, y: 4, z: 8, core: 2. Of those that a mesh axis runs over, the one named last changes fastest.
Arguments:
- params: float32 [59, 262144], P(None, 'row'), may hold values from -6 to 6, as said below
- first_moment: float32 [59, 262144], P(None, 'row'), may hold values from -6 to 6
- second_moment: float32 [59, 262144], P(None, 'row'), may hold values from 0.01 to 1
- camera: float32 [2, 4, 11], P(None, 'rep'), may hold values from -200 to 200, as said below
- tile_corner: float32 [2, 4, 256, 2], P(None, 'rep', 'row'), may hold values from 0 to 240
- tile_owner: int32 [2, 4, 256, 4], P(None, 'rep', 'row'), may hold values from 0 to 63, all different within a row; in each aligned block of 4 rows (0 to 3, 4 to 7, ..., all dimensions but the last counted through in order) at most 2 rows name the same one
- tile_block: int32 [2, 4, 256, 4], P(None, 'rep', 'row'), may hold values from 0 to 31
- depth_order: int32 [2, 4, 256, 512], P(None, 'rep', 'row'), may hold values from 0 to 511, each once within a row
- targets: float32 [2, 4, 256, 3, 256], P(None, 'rep', 'row'), may hold values from 0 to 1
- migration: int32 [64, 2, 2], P('row'), may hold values from 0 to 31, as said below
Outputs:
- new_params: float32 [59, 262144], P(None, 'row')
- new_first: float32 [59, 262144], P(None, 'row')
- new_second: float32 [59, 262144], P(None, 'row')
- rendered: float32 [2, 4, 256, 3, 256], P(None, 'rep', 'row')
The draws below stay inside these ranges and needn't reach their ends.
Inputs may be any that keep to these rules, and one draw needn't show every extreme that they name: `tile_owner`: each tile names 4 different owners; among the tiles of one device no owner is named more than 2 times. `depth_order`: each tile's row is a permutation. `migration`: the (4) entries of one owner are different blocks. `params`: row 6 lies in [1, 2]; rows 3 to 5 in [-1.9, -0.7]; row 10 in [2, 4]. `camera`: entries 8 to 10 form a unit vector.
All inputs are finite; a program needn't handle non-finite values.
Results may differ from the reference program's by a relative error of at most 0.0003.
Values sent between devices are 32-bit elements; how exact they have to be, the bound alone decides.
A program may use at most 64 MiB of HBM per device.

```python
import math
import jax
import jax.numpy as jnp
import numpy as np
from jax import lax

P_SIZE = 59
BLOCK = 128
LISTB = 4
PIX = 256
ITERS = 2
MIGH = 2
TILES_DEV = 4
BLK_DEV = 32
DEPTH = 512
OWNERS = 64
REPLICAS = 4
TILES = 256
GAUSS = 262144
CAP = 2


def draw_params(key, part):
    subkeys = jax.random.split(jax.random.fold_in(key, 101), 7)
    gauss_count = GAUSS
    means = jax.random.uniform(subkeys[0], (3, gauss_count), jnp.float32, -1.0, 1.0)
    log_scales = jax.random.uniform(subkeys[1], (3, gauss_count), jnp.float32, -1.9, -0.7)
    quat_real = jax.random.uniform(subkeys[2], (1, gauss_count), jnp.float32, 1.0, 2.0)
    quat_rest = jax.random.uniform(subkeys[3], (3, gauss_count), jnp.float32, -1.0, 1.0)
    logits = jax.random.uniform(subkeys[4], (1, gauss_count), jnp.float32, 2.0, 4.0)
    base_colour = jax.random.normal(subkeys[5], (3, gauss_count), jnp.float32)
    higher = 0.5 * jax.random.normal(subkeys[6], (45, gauss_count), jnp.float32)
    colour_rows = jnp.clip(jnp.concatenate([base_colour, higher], axis=0), -6.0, 6.0)
    return jnp.concatenate([means, log_scales, quat_real, quat_rest, logits, colour_rows], axis=0)


def draw_camera(key, part):
    subkeys = jax.random.split(jax.random.fold_in(key, 202), 4)
    affine = jnp.clip(50.0 * jax.random.normal(subkeys[0], (ITERS, REPLICAS, 6), jnp.float32), -200.0, 200.0)
    centre = 128.0 + jnp.clip(20.0 * jax.random.normal(subkeys[1], (ITERS, REPLICAS, 2), jnp.float32), -60.0, 60.0)
    height = jax.random.uniform(subkeys[2], (ITERS, REPLICAS, 1), jnp.float32, -1.0, 1.0)
    turning = jax.random.uniform(subkeys[3], (ITERS, REPLICAS, 1), jnp.float32, -jnp.pi, jnp.pi)
    radial = jnp.sqrt(1.0 - height * height)
    facing = jnp.concatenate([radial * jnp.cos(turning), radial * jnp.sin(turning), height], axis=-1)
    return jnp.concatenate([affine, centre, facing], axis=-1)


def draw_migration(key, part):
    subkeys = jax.random.split(jax.random.fold_in(key, 303), OWNERS)
    picks = jax.vmap(lambda k: jax.random.permutation(k, BLK_DEV)[:2 * MIGH])(subkeys)
    return picks.reshape(OWNERS, 2, MIGH).astype(jnp.int32)


def place_ends(result, rng, least, top_value):
    place = [jax.random.randint(jax.random.fold_in(rng, axis), (), 0, length) for axis, length in enumerate(result.shape)]
    main_axis = result.shape.index(max(result.shape))
    beside = place[:main_axis] + [(place[main_axis] + 1) % result.shape[main_axis]] + place[main_axis + 1:]
    return result.at[tuple(place)].set(least).at[tuple(beside)].set(top_value)


def level_of(key, dims, cuts, least, high):
    level, own = 1.0, jax.random.fold_in(key, 6)
    for dim, parts in cuts:
        steps = jnp.exp(jax.random.uniform(jax.random.fold_in(own, dim), (parts,), jnp.float32, least / len(cuts), high / len(cuts)))
        level = level * jnp.repeat(steps, dims[dim] // parts).reshape([-1 if axis == dim else 1 for axis in range(len(dims))])
    return level


def routed_block(stream_key, own, number, rows, count, top, limit, lean):
    order = jax.random.permutation(stream_key, count)
    heavy_load, common = load_shares(count, rows * top, limit, lean, True), load_shares(count, rows * top, limit, lean, False)
    places = jnp.arange(count)

    def named(lengths, turn):
        used = int((lengths > 0).sum())
        fixed = max(1, used // 4)
        passed = fixed + (places - fixed + turn * (used - fixed)) % max(1, count - fixed)
        return jnp.zeros((count,), jnp.int32).at[order[jnp.where(places < fixed, places, passed)]].set(jnp.asarray(lengths, jnp.int32))

    lengths = jnp.where(number % 4 == 0, named(heavy_load, number // 4), named(common, number - number // 4 - 1))
    mixed = jax.random.permutation(jax.random.fold_in(own, 3), count)
    giver, sink = mixed[0:count // 2 * 2:2], mixed[1:count // 2 * 2:2]
    room = jnp.minimum(lengths[giver] - 1, limit - lengths[sink]) // 2
    room = jnp.where((giver == order[0]) | (sink == order[0]) | (lengths[sink] == 0), 0, jnp.maximum(room, 0))
    passed = jax.random.randint(jax.random.fold_in(own, 4), (count // 2,), 0, 1 << 20) % (room + 1)
    lengths = lengths.at[giver].add(-passed).at[sink].add(passed)
    items = jnp.searchsorted(jnp.cumsum(lengths), jnp.arange(rows * top), side="right").astype(jnp.int32)
    listing = items.reshape(top, rows).T
    listing = listing[jax.random.permutation(jax.random.fold_in(own, 1), rows)]
    turn = jax.random.randint(jax.random.fold_in(own, 2), (rows, 1), 0, top)
    return jnp.take_along_axis(listing, (jnp.arange(top)[None, :] + turn) % top, axis=1)


def load_shares(number_of, total, most, lean, full):
    loads = [(1 << 20) // math.isqrt(standing ** lean) + 1 for standing in range(1, number_of + 1)]
    largest = most if full else min(most, max(-(-total // number_of), total * loads[0] // sum(loads)))
    least = 1 if total - largest >= number_of - 1 else 0
    counts, rest = [largest] + [least] * (number_of - 1), total - largest - least * (number_of - 1)
    while rest > 0:
        candidates = [i for i in range(1, number_of) if counts[i] < largest] or [i for i in range(1, number_of) if counts[i] < most]
        pool, budget = sum([loads[i] for i in candidates]), rest
        for i in candidates:
            addition = min(most - counts[i], max(1, budget * loads[i] // pool), rest)
            counts[i] = counts[i] + addition
            rest = rest - addition
    return np.array(counts)


def bell_draw(rng, extent, width, limit, cuts=(), kind=jnp.bfloat16):
    result = width * jax.random.normal(rng, extent, jnp.float32)
    if cuts:
        result = result * level_of(rng, extent, cuts, -0.22, 0.18)
    return jnp.clip(result, -limit, limit).astype(kind)


def setup_inputs(seed: int = 0) -> dict:
    keys = jax.random.split(jax.random.key(seed), 11)
    params = draw_params(jax.random.fold_in(keys[10], 71), 0)
    first_moment = bell_draw(keys[1], (P_SIZE, GAUSS), 1.0, 6.0, ((1, 64),), jnp.float32)
    second_moment = jnp.clip(jnp.exp(math.log(1.0) - 4.6051702 * jax.random.uniform(keys[2], (P_SIZE, GAUSS), jnp.float32) ** level_of(keys[2], (P_SIZE, GAUSS), ((1, 64),), -0.2, 0.2)), 0.01, 1.0)
    camera = draw_camera(jax.random.fold_in(keys[10], 71), 0)
    tile_corner = jnp.clip(240.0 * jax.random.uniform(keys[4], (ITERS, REPLICAS, TILES, 2), jnp.float32) ** level_of(keys[4], (ITERS, REPLICAS, TILES, 2), ((1, 4), (2, 64)), -0.2, 0.2), 0.0, 240.0)
    tile_owner_keys = jax.random.split(jax.random.fold_in(keys[5], 1), ITERS * REPLICAS * TILES // TILES_DEV)
    tile_owner_turns = jax.random.permutation(jax.random.fold_in(keys[5], 3), ITERS * REPLICAS * TILES // TILES_DEV)
    tile_owner = jax.vmap(lambda own, number: routed_block(jax.random.fold_in(keys[5], 2), own, number, TILES_DEV, OWNERS, LISTB, CAP, 2))(tile_owner_keys, tile_owner_turns).reshape((ITERS, REPLICAS, TILES, LISTB))
    tile_block = place_ends(jax.random.randint(keys[6], (ITERS, REPLICAS, TILES, LISTB), 0, BLK_DEV), jax.random.fold_in(keys[6], 1), 0, BLK_DEV - 1).astype(jnp.int32)
    depth_order = jax.vmap(lambda own: jax.random.permutation(own, DEPTH))(jax.random.split(keys[7], ITERS * REPLICAS * TILES)).reshape((ITERS, REPLICAS, TILES, DEPTH)).astype(jnp.int32)
    targets = jnp.clip(1.0 * jax.random.uniform(keys[8], (ITERS, REPLICAS, TILES, 3, PIX), jnp.float32) ** level_of(keys[8], (ITERS, REPLICAS, TILES, 3, PIX), ((1, 4), (2, 64)), -0.2, 0.2), 0.0, 1.0)
    migration = draw_migration(jax.random.fold_in(keys[10], 71), 0)
    return {"params": params, "first_moment": first_moment, "second_moment": second_moment, "camera": camera, "tile_corner": tile_corner, "tile_owner": tile_owner, "tile_block": tile_block, "depth_order": depth_order, "targets": targets, "migration": migration}


harm_zero = 0.28209479177387814
harm_one = 0.4886025119029199
harm_two = (1.0925484305920792, -1.0925484305920792, 0.31539156525252005, -1.0925484305920792, 0.5462742152960396)
harm_three = (-0.5900435899266435, 2.890611442640554, -0.4570457994644658, 0.3731763325901154, -0.4570457994644658, 1.445305721320277, -0.5900435899266435)
learn_rate = 0.01
adam_epsilon = 1e-08

def harmonics(facing):
    face_x, face_y, face_z = (facing[0], facing[1], facing[2])
    face_xx, face_yy, face_zz = (face_x * face_x, face_y * face_y, face_z * face_z)
    terms = [harm_zero + 0.0 * face_x, -harm_one * face_y, harm_one * face_z, -harm_one * face_x, harm_two[0] * face_x * face_y, harm_two[1] * face_y * face_z, harm_two[2] * (2.0 * face_zz - face_xx - face_yy), harm_two[3] * face_x * face_z, harm_two[4] * (face_xx - face_yy), harm_three[0] * face_y * (3.0 * face_xx - face_yy), harm_three[1] * face_x * face_y * face_z, harm_three[2] * face_y * (4.0 * face_zz - face_xx - face_yy), harm_three[3] * face_z * (2.0 * face_zz - 3.0 * face_xx - 3.0 * face_yy), harm_three[4] * face_x * (4.0 * face_zz - face_xx - face_yy), harm_three[5] * face_z * (face_xx - face_yy), harm_three[6] * face_x * (face_xx - 3.0 * face_yy)]
    return jnp.stack(terms)

def project(params, camera_now):
    means = params[0:3]
    scales = jnp.exp(params[3:6])
    quats = params[6:10]
    quats = quats / jnp.sqrt(lax.optimization_barrier(jnp.sum(quats * quats, axis=0, keepdims=True)))
    quat_w, quat_x, quat_y, quat_z = (quats[0], quats[1], quats[2], quats[3])
    rotation = [[1.0 - 2.0 * (quat_y * quat_y + quat_z * quat_z), 2.0 * (quat_x * quat_y - quat_w * quat_z), 2.0 * (quat_x * quat_z + quat_w * quat_y)], [2.0 * (quat_x * quat_y + quat_w * quat_z), 1.0 - 2.0 * (quat_x * quat_x + quat_z * quat_z), 2.0 * (quat_y * quat_z - quat_w * quat_x)], [2.0 * (quat_x * quat_z - quat_w * quat_y), 2.0 * (quat_y * quat_z + quat_w * quat_x), 1.0 - 2.0 * (quat_x * quat_x + quat_y * quat_y)]]
    affine = [[camera_now[0], camera_now[1], camera_now[2]], [camera_now[3], camera_now[4], camera_now[5]]]
    spread = [[(affine[i][0] * rotation[0][k] + affine[i][1] * rotation[1][k] + affine[i][2] * rotation[2][k]) * scales[k] for k in range(3)] for i in range(2)]
    cov_xx = spread[0][0] * spread[0][0] + spread[0][1] * spread[0][1] + spread[0][2] * spread[0][2] + 0.3
    cov_yy = spread[1][0] * spread[1][0] + spread[1][1] * spread[1][1] + spread[1][2] * spread[1][2] + 0.3
    cov_xy = spread[0][0] * spread[1][0] + spread[0][1] * spread[1][1] + spread[0][2] * spread[1][2]
    determinant = cov_xx * cov_yy - cov_xy * cov_xy
    centre_x = affine[0][0] * means[0] + affine[0][1] * means[1] + affine[0][2] * means[2] + camera_now[6]
    centre_y = affine[1][0] * means[0] + affine[1][1] * means[1] + affine[1][2] * means[2] + camera_now[7]
    basis = harmonics(camera_now[8:11])
    colours = 0.5 + jnp.einsum('k,kcg->cg', basis, params[11:59].reshape(16, 3, -1), precision=lax.Precision.HIGHEST)
    opacity = jax.nn.sigmoid(params[10])
    geometry = jnp.stack([centre_x, centre_y, cov_yy / determinant, -cov_xy / determinant, cov_xx / determinant])
    return jnp.concatenate([geometry, colours, opacity[None]], axis=0)

def render(splat_rows, corner):
    side = math.isqrt(PIX)
    pixels = jnp.arange(PIX, dtype=jnp.int32)
    pos_x = corner[0] + (pixels % side).astype(jnp.float32) + 0.5
    pos_y = corner[1] + (pixels // side).astype(jnp.float32) + 0.5
    gap_x = pos_x[:, None] - splat_rows[0][None, :]
    gap_y = pos_y[:, None] - splat_rows[1][None, :]
    exponent = 0.5 * (splat_rows[2] * gap_x * gap_x + 2.0 * splat_rows[3] * gap_x * gap_y + splat_rows[4] * gap_y * gap_y)
    alphas = splat_rows[8] * jnp.exp(-exponent)
    log_keep = jnp.log1p(-alphas)
    transmit = jnp.exp(jnp.cumsum(log_keep, axis=1) - log_keep)
    return jnp.einsum('cn,pn->cp', splat_rows[5:8], alphas * transmit, precision=lax.Precision.HIGHEST)

def reference(params, first_moment, second_moment, camera, tile_corner, tile_owner, tile_block, depth_order, targets, migration):
    offsets = jnp.arange(BLOCK, dtype=jnp.int32)
    current = params
    moment_one = first_moment
    moment_two = second_moment
    pictures = []
    for step_index in range(ITERS):
        gradient = jnp.zeros_like(current)
        frames = []
        for replica in range(REPLICAS):
            camera_now = camera[step_index, replica]
            projected, pullback = jax.vjp(lambda p: project(p, camera_now), current)
            firsts = (tile_owner[step_index, replica] * BLK_DEV + tile_block[step_index, replica]) * BLOCK
            gauss_ids = (firsts[:, :, None] + offsets[None, None, :]).reshape(TILES, DEPTH).astype(jnp.int32)
            ordered = jnp.take_along_axis(gauss_ids, depth_order[step_index, replica], axis=1)

            def one_tile(pieces):
                tile_ids, corner, target = pieces
                splat_rows = jnp.take(projected, tile_ids, axis=1)
                picture, tile_back = jax.vjp(lambda r: render(r, corner), splat_rows)
                return (picture, tile_back(picture - target)[0])
            picture, tile_grads = lax.map(one_tile, (ordered, tile_corner[step_index, replica], targets[step_index, replica]))
            flat_grads = jnp.transpose(tile_grads, (1, 0, 2)).reshape(9, TILES * DEPTH)
            row_grads = jnp.zeros_like(projected).at[:, ordered.reshape(-1)].add(flat_grads)
            gradient = gradient + pullback(row_grads)[0]
            frames.append(picture)
        pictures.append(jnp.stack(frames))
        moment_one = 0.9 * moment_one + 0.1 * gradient
        moment_two = 0.999 * moment_two + 0.001 * gradient * gradient
        current = current - learn_rate * moment_one / (jnp.sqrt(moment_two) + adam_epsilon)
    stacked = jnp.stack([current, moment_one, moment_two]).reshape(3, P_SIZE, OWNERS, BLK_DEV, BLOCK)
    owner_ids = jnp.arange(OWNERS, dtype=jnp.int32)
    moved = stacked
    for column in range(MIGH):
        going_left = migration[:, 0, column]
        going_right = migration[:, 1, column]
        from_left = jnp.roll(stacked[:, :, owner_ids, going_right], 1, axis=2)
        from_right = jnp.roll(stacked[:, :, owner_ids, going_left], -1, axis=2)
        moved = moved.at[:, :, owner_ids, going_left].set(from_left)
        moved = moved.at[:, :, owner_ids, going_right].set(from_right)
    moved = moved.reshape(3, P_SIZE, GAUSS)
    return (moved[0], moved[1], moved[2], jnp.stack(pictures))
```

```python
import functools

import jax
import jax.numpy as jnp
from jax import lax
from jax.experimental import pallas as pl
from jax.experimental.pallas import tpu as pltpu
from jax.sharding import PartitionSpec as P

P_SIZE = 59
BLOCK = 128
LISTB = 4
PIX = 256
SIDE = 16
ITERS = 2
MIGH = 2
DEPTH = 512
NINE = 9
CAP = 2
STRIDE = 64
PAIR = 24
SENT = 18
MESH = pl.DeviceIdType.MESH
f32 = jnp.float32
bf16 = jnp.bfloat16

harm_zero = 0.28209479177387814
harm_one = 0.4886025119029199
harm_two = (
    1.0925484305920792,
    -1.0925484305920792,
    0.31539156525252005,
    -1.0925484305920792,
    0.5462742152960396,
)
harm_three = (
    -0.5900435899266435,
    2.890611442640554,
    -0.4570457994644658,
    0.3731763325901154,
    -0.4570457994644658,
    1.445305721320277,
    -0.5900435899266435,
)
learn_rate = 0.01
adam_epsilon = 1e-08


def harmonics(face_x, face_y, face_z):
    face_xx, face_yy, face_zz = (face_x * face_x, face_y * face_y, face_z * face_z)
    return [
        harm_zero + 0.0 * face_x,
        -harm_one * face_y,
        harm_one * face_z,
        -harm_one * face_x,
        harm_two[0] * face_x * face_y,
        harm_two[1] * face_y * face_z,
        harm_two[2] * (2.0 * face_zz - face_xx - face_yy),
        harm_two[3] * face_x * face_z,
        harm_two[4] * (face_xx - face_yy),
        harm_three[0] * face_y * (3.0 * face_xx - face_yy),
        harm_three[1] * face_x * face_y * face_z,
        harm_three[2] * face_y * (4.0 * face_zz - face_xx - face_yy),
        harm_three[3] * face_z * (2.0 * face_zz - 3.0 * face_xx - 3.0 * face_yy),
        harm_three[4] * face_x * (4.0 * face_zz - face_xx - face_yy),
        harm_three[5] * face_z * (face_xx - face_yy),
        harm_three[6] * face_x * (face_xx - 3.0 * face_yy),
    ]


def split2(x):
    high = x.astype(bf16)
    return high, (x - high.astype(f32)).astype(bf16)


def split3(x):
    high = x.astype(bf16)
    rest = x - high.astype(f32)
    mid = rest.astype(bf16)
    return high, mid, (rest - mid.astype(f32)).astype(bf16)


def dot(a, b, dims=((1,), (0,))):
    return lax.dot_general(a, b, (dims, ((), ())), preferred_element_type=f32)


NT = ((1,), (1,))


def geometry(rows):
    scales = [jnp.exp(rows(3 + k)) for k in range(3)]
    q = [rows(6 + k) for k in range(4)]
    inverse = 1.0 / jnp.sqrt(q[0] * q[0] + q[1] * q[1] + q[2] * q[2] + q[3] * q[3])
    w, x, y, z = [v * inverse for v in q]
    rotation = [
        [1.0 - 2.0 * (y * y + z * z), 2.0 * (x * y - w * z), 2.0 * (x * z + w * y)],
        [2.0 * (x * y + w * z), 1.0 - 2.0 * (x * x + z * z), 2.0 * (y * z - w * x)],
        [2.0 * (x * z - w * y), 2.0 * (y * z + w * x), 1.0 - 2.0 * (x * x + y * y)],
    ]
    return scales, (w, x, y, z), inverse, rotation


def conic_of(affine, scales, rotation):
    spread = [
        [
            (affine[i][0] * rotation[0][k] + affine[i][1] * rotation[1][k] + affine[i][2] * rotation[2][k])
            * scales[k]
            for k in range(3)
        ]
        for i in range(2)
    ]
    s0, s1 = spread
    cov_xx = s0[0] * s0[0] + s0[1] * s0[1] + s0[2] * s0[2] + 0.3
    cov_yy = s1[0] * s1[0] + s1[1] * s1[1] + s1[2] * s1[2] + 0.3
    cov_xy = s0[0] * s1[0] + s0[1] * s1[1] + s0[2] * s1[2]
    over = 1.0 / (cov_xx * cov_yy - cov_xy * cov_xy)
    return spread, (cov_yy * over, -cov_xy * over, cov_xx * over)


def sigmoid(x):
    return 1.0 / (1.0 + jnp.exp(-x))


def kernel(
    nr,
    nx,
    nb,
    tiles,
    corner_ref,
    own_ref,
    migration_ref,
    request_ref,
    column_ref,
    camera_ref,
    order_ref,
    target_ref,
    p_hbm,
    m_hbm,
    v_hbm,
    p_out,
    m_out,
    v_out,
    picture_ref,
    p_s,
    m_s,
    v_s,
    ask_send,
    ask_recv,
    cam_recv,
    cam_smem,
    f_send,
    f_recv,
    g_send,
    g_recv,
    shared,
    mig_send,
    mig_recv,
    listing,
    listed_rows,
    picks,
    upper,
    lower,
    logs,
    alphas,
    passing,
    weight_high,
    weight_low,
    pulls,
    products,
    behind,
    request_grads,
    local_sem,
    out_sem,
    ask_ssem,
    ask_rsem,
    cam_ssem,
    cam_rsem,
    cam_sem,
    a2a_ssem,
    a2a_rsem,
    rep_ssem,
    rep_rsem,
    mig_ssem,
    mig_rsem,
):
    me = lax.axis_index("row")
    rep = lax.axis_index("rep")
    state = (p_s, m_s, v_s)

    def block_rows(ref, b):
        return ref.at[pl.ds(pl.multiple_of(STRIDE * b, 8), P_SIZE), :]

    def lanes_of(ref, b):
        return ref.at[:, pl.ds(pl.multiple_of(BLOCK * b, BLOCK), BLOCK)]

    def load_copy(a, b):
        return pltpu.make_async_copy(
            lanes_of((p_hbm, m_hbm, v_hbm)[a], b), block_rows(state[a], b), local_sem.at[a, b]
        )

    for a in range(3):
        lax.fori_loop(0, nb, lambda b, c: (load_copy(a, b).start(), c)[1], 0)

    barrier = pltpu.get_barrier_semaphore()

    def greet_row(k, c):
        pl.semaphore_signal(barrier, 1, device_id={"row": lax.rem(me + k, nr)}, device_id_type=MESH)
        return c

    def greet_rep(k, c):
        pl.semaphore_signal(barrier, 1, device_id={"rep": lax.rem(rep + k, nx)}, device_id_type=MESH)
        return c

    lax.fori_loop(1, nr, greet_row, 0)
    lax.fori_loop(1, nx, greet_rep, 0)

    asked_now = jnp.full((nr, BLOCK), -1, jnp.int32)
    lane = lax.broadcasted_iota(jnp.int32, (nr, BLOCK), 1)
    owner_id = lax.broadcasted_iota(jnp.int32, (nr, BLOCK), 0)
    requests = tiles * LISTB
    for i in range(ITERS):
        for s in range(CAP):
            match = (owner_id * CAP + s == request_ref[i : i + 1, :]) & (lane < requests)
            column = jnp.sum(
                jnp.where(match, request_ref[ITERS + i : ITERS + i + 1, :] + 1.0, 0.0), axis=1, keepdims=True
            )
            asked_now = jnp.where(lane == CAP * i + s, column.astype(jnp.int32) - 1, asked_now)
    ask_send[pl.ds(0, nr, stride=8), :] = asked_now
    cam_recv[pl.ds(pl.multiple_of(8 * rep, 8), 1), :] = camera_ref[...]

    pl.semaphore_wait(barrier, nr + nx - 2)

    def row_of(k):
        return lax.rem(me + k, nr), lax.rem(me + nr - k, nr)

    def ask_copy(k, at):
        to, _ = row_of(k)
        return pltpu.make_async_remote_copy(
            src_ref=ask_send.at[pl.ds(pl.multiple_of(8 * to, 8), 1), :],
            dst_ref=ask_recv.at[pl.ds(pl.multiple_of(8 * at, 8), 1), :],
            send_sem=ask_ssem.at[k],
            recv_sem=ask_rsem.at[k],
            device_id={"row": to},
            device_id_type=MESH,
        )

    def cam_copy(k, at):
        return pltpu.make_async_remote_copy(
            src_ref=cam_recv.at[pl.ds(pl.multiple_of(8 * rep, 8), 1), :],
            dst_ref=cam_recv.at[pl.ds(pl.multiple_of(8 * at, 8), 1), :],
            send_sem=cam_ssem.at[k],
            recv_sem=cam_rsem.at[k],
            device_id={"rep": lax.rem(rep + k, nx)},
            device_id_type=MESH,
        )

    lax.fori_loop(1, nr, lambda k, c: (ask_copy(k, me).start(), c)[1], 0)
    for k in range(1, nx):
        cam_copy(k, rep).start()
    own_ask = pl.ds(pl.multiple_of(8 * me, 8), 8)
    ask_recv[own_ask, :] = ask_send[own_ask, :]

    square = lax.broadcasted_iota(jnp.int32, (DEPTH, DEPTH), 0), lax.broadcasted_iota(jnp.int32, (DEPTH, DEPTH), 1)
    before = jnp.where(square[0] < square[1], 1.0, 0.0).astype(bf16)
    after = jnp.where(square[0] > square[1], 1.0, 0.0).astype(bf16)
    for part in range(3):
        upper[part * DEPTH : (part + 1) * DEPTH, :] = before
    for part in range(2):
        lower[part * DEPTH : (part + 1) * DEPTH, :] = after
    listed_rows[...] = jnp.zeros_like(listed_rows)

    for a in range(3):
        lax.fori_loop(0, nb, lambda b, c: (load_copy(a, b).wait(), c)[1], 0)

    def row(ref, r):
        return ref[pl.ds(r, nb, stride=STRIDE), :]

    def put_row(ref, r, x):
        ref[pl.ds(r, nb, stride=STRIDE), :] = x

    def project(i):
        cam = [own_ref[i, k] for k in range(11)]
        affine = [cam[0:3], cam[3:6]]
        rows = functools.partial(row, p_s)
        scales, _, _, rotation = geometry(rows)
        _, conic = conic_of(affine, scales, rotation)
        means = [rows(k) for k in range(3)]
        centre = [
            affine[j][0] * means[0] + affine[j][1] * means[1] + affine[j][2] * means[2] + cam[6 + j] for j in range(2)
        ]
        basis = harmonics(*cam[8:11])
        colours = []
        for k in range(3):
            total = basis[0] * rows(11 + k)
            for j in range(1, 16):
                total = total + basis[j] * rows(11 + 3 * j + k)
            colours.append(0.5 + total)
        return centre + list(conic) + colours + [sigmoid(rows(10))]

    def put_slots(ref, values):
        for s in range(CAP):
            for c in range(NINE):
                base = 8 * s + c if c < 8 else 16 + s
                ref[pl.ds(base, nr, stride=PAIR), :] = values[s * nr : (s + 1) * nr, c * BLOCK : (c + 1) * BLOCK]

    def get_slots(ref):
        columns = []
        for c in range(NINE):
            columns.append(
                jnp.concatenate(
                    [ref[pl.ds(8 * s + c if c < 8 else 16 + s, nr, stride=PAIR), :] for s in range(CAP)], axis=0
                )
            )
        return jnp.concatenate(columns, axis=1)

    def pair_rows(p):
        return pl.ds(pl.multiple_of(PAIR * p, 8), SENT)

    def slot_copy(send, recv, which, k, at):
        to, _ = row_of(k)
        return pltpu.make_async_remote_copy(
            src_ref=send.at[pair_rows(to), :],
            dst_ref=recv.at[pair_rows(at), :],
            send_sem=a2a_ssem.at[which, k],
            recv_sem=a2a_rsem.at[which, k],
            device_id={"row": to},
            device_id_type=MESH,
        )

    def exchange(send, recv, which):
        lax.fori_loop(1, nr, lambda k, c: (slot_copy(send, recv, which, k, me).start(), c)[1], 0)
        own = pl.ds(pl.multiple_of(PAIR * me, 8), PAIR)
        recv[own, :] = send[own, :]

        def arrived(k, c):
            copy = slot_copy(send, recv, which, k, row_of(k)[1])
            copy.wait_recv()
            copy.wait_send()
            return c

        lax.fori_loop(1, nr, arrived, 0)

    def render(i, recv):
        slot_lane = lax.broadcasted_iota(jnp.int32, (requests, CAP * nr), 1)
        slot_lane = CAP * lax.rem(slot_lane, nr) + slot_lane // nr
        take = jnp.where(column_ref[:, i : i + 1] == slot_lane.astype(f32), 1.0, 0.0).astype(bf16)
        pieces = split3(get_slots(recv))
        listed = dot(take, pieces[0]) + dot(take, pieces[1]) + dot(take, pieces[2])
        for c in range(NINE):
            listed_rows[pl.ds(c, requests, stride=16), :] = listed[:, BLOCK * c : BLOCK * (c + 1)]

        def one_tile(t, carry):
            for j in range(LISTB):
                listing[:, BLOCK * j : BLOCK * (j + 1)] = listed_rows[
                    pl.ds(pl.multiple_of(16 * (LISTB * t + j), 16), 16), :
                ]
            order = order_ref[pl.ds(i * tiles + t, 1), 0, :]
            pick = jnp.where(lax.broadcasted_iota(jnp.int32, (DEPTH, DEPTH), 0) == order, 1.0, 0.0).astype(bf16)
            picks[...] = pick
            parts = dot(jnp.concatenate(split3(listing[...]), axis=0), picks[...])
            splats = parts[0:16] + parts[16:32] + parts[32:48]
            centre_x, centre_y = splats[0:1], splats[1:2]
            conic_a, conic_b, conic_c = splats[2:3], splats[3:4], splats[4:5]
            opacity = splats[8:9]
            ticks = lax.broadcasted_iota(jnp.int32, (SIDE, DEPTH), 0).astype(f32)
            gap_x = (corner_ref[i, 2 * t] + ticks + 0.5) - centre_x
            gap_y = (corner_ref[i, 2 * t + 1] + ticks + 0.5) - centre_y
            along = -0.5 * conic_a * gap_x * gap_x
            cross = -conic_b * gap_y
            across = -0.5 * conic_c * gap_y * gap_y
            for y in range(SIDE):
                at = slice(SIDE * y, SIDE * (y + 1))
                alpha = opacity * jnp.exp(along + across[y : y + 1] + gap_x * cross[y : y + 1])
                alphas[at, :] = alpha
                for part, piece in enumerate(split3(jnp.log(1.0 - alpha))):
                    logs[at, part * DEPTH : (part + 1) * DEPTH] = piece
            passing[...] = dot(logs[...], upper[...])
            for y in range(SIDE):
                at = slice(SIDE * y, SIDE * (y + 1))
                through = jnp.exp(passing[at, :])
                passing[at, :] = through
                high, low = split2(alphas[at, :] * through)
                weight_high[at, :] = high
                weight_low[at, :] = low
            eight = lax.broadcasted_iota(jnp.int32, (8, 1), 0)
            paint = jnp.where(eight >= 5, splats[0:8], 0.0)
            paint_high = paint.astype(bf16).astype(f32)
            paint_low = paint - paint_high
            both = dot(jnp.concatenate([paint_high, paint_low], axis=0).astype(bf16), weight_high[...], NT)
            high_low = dot(jnp.concatenate([paint_high, paint_high], axis=0).astype(bf16), weight_low[...], NT)
            picture = both[0:8] + both[8:16] + high_low[0:8]
            picture_ref[i * tiles + t] = picture[5:8]
            residual = picture - jnp.concatenate([jnp.zeros((5, PIX), f32), target_ref[i * tiles + t]], axis=0)
            res_high = residual.astype(bf16).astype(f32)
            res_low = residual - res_high
            pull = dot(
                jnp.transpose(jnp.concatenate([res_high, res_high, res_low, res_low], axis=0)).astype(bf16),
                jnp.concatenate([paint_high, paint_low, paint_high, paint_low], axis=0).astype(bf16),
            )
            pulls[...] = pull
            both = dot(jnp.concatenate([res_high, res_low], axis=0).astype(bf16), weight_high[...])
            high_low = dot(jnp.concatenate([res_high, res_high], axis=0).astype(bf16), weight_low[...])
            colour_grads = both[0:8] + both[8:16] + high_low[0:8]
            for y in range(SIDE):
                at = slice(SIDE * y, SIDE * (y + 1))
                for part, piece in enumerate(split2(alphas[at, :] * passing[at, :] * pulls[at, :])):
                    products[at, part * DEPTH : (part + 1) * DEPTH] = piece
            behind[...] = dot(products[...], lower[...])
            sums = [jnp.zeros((SIDE, DEPTH), f32) for _ in range(3)]
            for y in range(SIDE):
                at = slice(SIDE * y, SIDE * (y + 1))
                alpha = alphas[at, :]
                felt = alpha * (passing[at, :] * pulls[at, :] - behind[at, :] / (1.0 - alpha))
                tall = felt * gap_y[y : y + 1]
                sums = [sums[0] + felt, sums[1] + tall, sums[2] + tall * gap_y[y : y + 1]]

            def over_x(v):
                return jnp.sum(v, axis=0, keepdims=True)

            felt_x = gap_x * sums[0]
            total, total_x, total_xx = over_x(sums[0]), over_x(felt_x), over_x(gap_x * felt_x)
            total_y, total_xy, total_yy = over_x(sums[1]), over_x(gap_x * sums[1]), over_x(sums[2])
            grads = jnp.concatenate(
                [
                    conic_a * total_x + conic_b * total_y,
                    conic_b * total_x + conic_c * total_y,
                    -0.5 * total_xx,
                    -total_xy,
                    -0.5 * total_yy,
                    colour_grads[5:8],
                    total / opacity,
                    jnp.zeros((7, DEPTH), f32),
                ],
                axis=0,
            )
            parts = dot(jnp.concatenate(split3(grads), axis=0), picks[...], NT)
            listed = parts[0:16] + parts[16:32] + parts[32:48]
            for j in range(LISTB):
                request_grads[pl.ds(pl.multiple_of(16 * (LISTB * t + j), 16), 16), :] = listed[
                    :, BLOCK * j : BLOCK * (j + 1)
                ]
            return carry

        lax.fori_loop(0, tiles, one_tile, 0)

    def step_up(r, gradient):
        one = 0.9 * row(m_s, r) + 0.1 * gradient
        two = 0.999 * row(v_s, r) + 0.001 * gradient * gradient
        put_row(m_s, r, one)
        put_row(v_s, r, two)
        put_row(p_s, r, row(p_s, r) - learn_rate * one / (jnp.sqrt(two) + adam_epsilon))

    def pull_back(i, shares):
        rows = functools.partial(row, p_s)
        scales, quats, inverse, rotation = geometry(rows)
        cams = [[cam_smem[8 * x, 11 * i + k] for k in range(11)] for x in range(nx)]
        turn = None
        for x in range(nx):
            cam = cams[x]
            affine = [cam[0:3], cam[3:6]]

            def share(c):
                at = (x * NINE + c) * nb
                return shares[at : at + nb, :]

            spread, (con_a, con_b, con_c) = conic_of(affine, scales, rotation)
            g_a, g_b, g_c = share(2), 0.5 * share(3), share(4)
            left_a, left_b = g_a * con_a + g_b * con_b, g_a * con_b + g_b * con_c
            right_a, right_b = g_b * con_a + g_c * con_b, g_b * con_b + g_c * con_c
            n_xx = -2.0 * (con_a * left_a + con_b * right_a)
            n_xy = -2.0 * (con_a * left_b + con_b * right_b)
            n_yy = -2.0 * (con_b * left_b + con_c * right_b)
            felt = [
                [n_xx * spread[0][k] + n_xy * spread[1][k] for k in range(3)],
                [n_xy * spread[0][k] + n_yy * spread[1][k] for k in range(3)],
            ]
            stretch = [felt[0][k] * spread[0][k] + felt[1][k] * spread[1][k] for k in range(3)]
            twist = [
                [(affine[0][j] * felt[0][k] + affine[1][j] * felt[1][k]) * scales[k] for k in range(3)]
                for j in range(3)
            ]
            moved = [affine[0][j] * share(0) + affine[1][j] * share(1) for j in range(3)]
            fade = share(8)
            if turn is None:
                stretches, turn, moves, fades = stretch, twist, moved, fade
            else:
                stretches = [u + v for u, v in zip(stretches, stretch)]
                turn = [[u + v for u, v in zip(a, b)] for a, b in zip(turn, twist)]
                moves = [u + v for u, v in zip(moves, moved)]
                fades = fades + fade
        w, x, y, z = quats
        d = turn
        unit = [
            2.0 * (z * (d[1][0] - d[0][1]) + y * (d[0][2] - d[2][0]) + x * (d[2][1] - d[1][2])),
            2.0
            * (
                y * (d[0][1] + d[1][0])
                + z * (d[0][2] + d[2][0])
                + w * (d[2][1] - d[1][2])
                - 2.0 * x * (d[1][1] + d[2][2])
            ),
            2.0
            * (
                x * (d[0][1] + d[1][0])
                + w * (d[0][2] - d[2][0])
                + z * (d[1][2] + d[2][1])
                - 2.0 * y * (d[0][0] + d[2][2])
            ),
            2.0
            * (
                w * (d[1][0] - d[0][1])
                + x * (d[0][2] + d[2][0])
                + y * (d[1][2] + d[2][1])
                - 2.0 * z * (d[0][0] + d[1][1])
            ),
        ]
        inner = unit[0] * w + unit[1] * x + unit[2] * y + unit[3] * z
        opacity = sigmoid(rows(10))
        for k in range(3):
            step_up(k, moves[k])
        for k in range(3):
            step_up(3 + k, stretches[k])
        for k in range(4):
            step_up(6 + k, (unit[k] - quats[k] * inner) * inverse)
        step_up(10, fades * opacity * (1.0 - opacity))
        bases = [harmonics(*cam[8:11]) for cam in cams]
        for k in range(3):
            felt = [shares[(x * NINE + 5 + k) * nb : (x * NINE + 6 + k) * nb, :] for x in range(nx)]
            for j in range(16):
                total = bases[0][j] * felt[0]
                for x in range(1, nx):
                    total = total + bases[x][j] * felt[x]
                step_up(11 + 3 * j + k, total)

    def share_copy(i, k, at):
        size = NINE * nb
        return pltpu.make_async_remote_copy(
            src_ref=shared.at[i, pl.ds(pl.multiple_of(size * rep, 8), size), :],
            dst_ref=shared.at[i, pl.ds(pl.multiple_of(size * at, 8), size), :],
            send_sem=rep_ssem.at[i, k],
            recv_sem=rep_rsem.at[i, k],
            device_id={"rep": lax.rem(rep + k, nx)},
            device_id_type=MESH,
        )

    asked_columns = asked_lines = None
    for i in range(ITERS):
        projected = jnp.concatenate(project(i), axis=1)
        if i == 0:

            def asked(k, c):
                copy = ask_copy(k, row_of(k)[1])
                copy.wait_recv()
                copy.wait_send()
                return c

            lax.fori_loop(1, nr, asked, 0)
            asked_all = ask_recv[pl.ds(0, nr, stride=8), :].astype(f32)
            asked_columns = asked_all
            asked_lines = jnp.transpose(
                asked_all
                if nr == BLOCK
                else jnp.concatenate([asked_all, jnp.zeros((BLOCK - nr, BLOCK), f32)], axis=0)
            )
        block_lane = lax.rem(lax.broadcasted_iota(jnp.int32, (nr, 3 * nb), 1), nb).astype(f32)
        serve = jnp.concatenate(
            [
                jnp.where(asked_columns[:, CAP * i + s : CAP * i + s + 1] == block_lane, 1.0, 0.0)
                for s in range(CAP)
            ],
            axis=0,
        ).astype(bf16)
        put_slots(f_send.at[i], dot(serve, jnp.concatenate(split3(projected), axis=0)))
        exchange(f_send.at[i], f_recv.at[i], 2 * i)
        render(i, f_recv.at[i])
        by_request = jnp.concatenate([request_grads[pl.ds(c, requests, stride=16), :] for c in range(NINE)], axis=1)
        slot_line = lax.broadcasted_iota(jnp.int32, (CAP * nr, 3 * requests), 0)
        slot_line = CAP * lax.rem(slot_line, nr) + slot_line // nr
        back = jnp.where(slot_line.astype(f32) == request_ref[i : i + 1, 0 : 3 * requests], 1.0, 0.0).astype(bf16)
        put_slots(g_send.at[i], dot(back, jnp.concatenate(split3(by_request), axis=0)))
        exchange(g_send.at[i], g_recv.at[i], 2 * i + 1)
        wanted = jnp.concatenate(
            [asked_lines[CAP * i + s : CAP * i + s + 1, 0:nr] for s in range(CAP)], axis=1
        )
        gather = jnp.where(
            lax.broadcasted_iota(jnp.int32, (nb, CAP * nr), 0).astype(f32) == wanted, 1.0, 0.0
        ).astype(bf16)
        pieces = split3(get_slots(g_recv.at[i]))
        summed = dot(gather, pieces[0]) + dot(gather, pieces[1]) + dot(gather, pieces[2])
        for c in range(NINE):
            shared[i, pl.ds(pl.multiple_of(NINE * nb * rep + nb * c, 8), nb), :] = summed[
                :, BLOCK * c : BLOCK * (c + 1)
            ]
        for k in range(1, nx):
            share_copy(i, k, rep).start()
        if i == 0:
            for k in range(1, nx):
                copy = cam_copy(k, lax.rem(rep + nx - k, nx))
                copy.wait_recv()
                copy.wait_send()
            table = pltpu.make_async_copy(cam_recv, cam_smem, cam_sem)
            table.start()
            table.wait()
        for k in range(1, nx):
            copy = share_copy(i, k, lax.rem(rep + nx - k, nx))
            copy.wait_recv()
            copy.wait_send()
        pull_back(i, shared.at[i])

    hand = MIGH * 3 * STRIDE

    def hand_copy(side):
        to = lax.rem(me + (nr - 1 if side == 0 else 1), nr)
        return pltpu.make_async_remote_copy(
            src_ref=mig_send.at[pl.ds(side * hand, hand), :],
            dst_ref=mig_recv.at[pl.ds((1 - side) * hand, hand), :],
            send_sem=mig_ssem.at[side],
            recv_sem=mig_rsem.at[side],
            device_id={"row": to},
            device_id_type=MESH,
        )

    for side in range(2):
        for j in range(MIGH):
            leaving = jnp.full((STRIDE, BLOCK), migration_ref[side, j], jnp.int32)
            for a in range(3):
                at = side * hand + (3 * j + a) * STRIDE
                chosen = state[a][0:STRIDE, :]
                for b in range(1, nb):
                    chosen = jnp.where(leaving == b, state[a][STRIDE * b : STRIDE * (b + 1), :], chosen)
                mig_send[at : at + STRIDE, :] = chosen
        hand_copy(side).start()
    for side in range(2):
        hand_copy(side).wait_recv()
        hand_copy(side).wait_send()

    def settle(b, carry):
        for a in range(3):
            at = pl.ds(pl.multiple_of(STRIDE * b, STRIDE), STRIDE)
            block = state[a][at, :]
            for side in range(2):
                for j in range(MIGH):
                    source = side * hand + (3 * j + a) * STRIDE
                    here = jnp.full((STRIDE, BLOCK), migration_ref[side, j], jnp.int32) == b
                    block = jnp.where(here, mig_recv[source : source + STRIDE, :], block)
            state[a][at, :] = block
            store_copy(a, b).start()
        return carry

    def store_copy(a, b):
        return pltpu.make_async_copy(
            block_rows(state[a], b), lanes_of((p_out, m_out, v_out)[a], b), out_sem.at[a, b]
        )

    lax.fori_loop(0, nb, settle, 0)
    for a in range(3):
        lax.fori_loop(0, nb, lambda b, c: (store_copy(a, b).wait(), c)[1], 0)


def local(
    params,
    first_moment,
    second_moment,
    camera,
    tile_corner,
    tile_owner,
    tile_block,
    depth_order,
    targets,
    migration,
):
    nr, nx = lax.axis_size("row"), lax.axis_size("rep")
    local_gauss = params.shape[1]
    nb = local_gauss // BLOCK
    tiles = tile_owner.shape[2]
    requests = tiles * LISTB
    owner = tile_owner.reshape(ITERS, requests)
    block = tile_block.reshape(ITERS, requests)
    position = jnp.arange(requests, dtype=jnp.int32)
    same = (owner[:, :, None] == owner[:, None, :]) & (position[None, :] < position[:, None])
    slot = owner * CAP + jnp.sum(same.astype(jnp.int32), axis=2)
    wide = jnp.concatenate([slot, slot, slot], axis=1).astype(f32)
    table = jnp.concatenate(
        [
            jnp.pad(wide, ((0, 0), (0, BLOCK - 3 * requests)), constant_values=-1.0),
            jnp.pad(block.astype(f32), ((0, 0), (0, BLOCK - requests))),
            jnp.zeros((8 - 2 * ITERS, BLOCK), f32),
        ],
        axis=0,
    )
    own = camera.reshape(ITERS, 11)
    packed = jnp.pad(own.reshape(1, ITERS * 11), ((0, 0), (0, BLOCK - ITERS * 11)))

    vmem = pl.BlockSpec(memory_space=pltpu.VMEM)
    smem = pl.BlockSpec(memory_space=pltpu.SMEM)
    hbm = pl.BlockSpec(memory_space=pl.ANY)
    size = jax.ShapeDtypeStruct((P_SIZE, local_gauss), f32)
    dma = pltpu.SemaphoreType.DMA
    new_params, new_first, new_second, pictures = pl.pallas_call(
        functools.partial(kernel, nr, nx, nb, tiles),
        out_shape=(size, size, size, jax.ShapeDtypeStruct((ITERS * tiles, 3, PIX), f32)),
        in_specs=[smem] * 3 + [vmem] * 5 + [hbm] * 3,
        out_specs=(hbm, hbm, hbm, vmem),
        scratch_shapes=[
            pltpu.VMEM((STRIDE * nb, BLOCK), f32),
            pltpu.VMEM((STRIDE * nb, BLOCK), f32),
            pltpu.VMEM((STRIDE * nb, BLOCK), f32),
            pltpu.VMEM((8 * nr, BLOCK), jnp.int32),
            pltpu.VMEM((8 * nr, BLOCK), jnp.int32),
            pltpu.VMEM((8 * nx, BLOCK), f32),
            pltpu.SMEM((8 * nx, BLOCK), f32),
            pltpu.VMEM((ITERS, PAIR * nr, BLOCK), f32),
            pltpu.VMEM((ITERS, PAIR * nr, BLOCK), f32),
            pltpu.VMEM((ITERS, PAIR * nr, BLOCK), f32),
            pltpu.VMEM((ITERS, PAIR * nr, BLOCK), f32),
            pltpu.VMEM((ITERS, nx * NINE * nb, BLOCK), f32),
            pltpu.VMEM((2 * MIGH * 3 * STRIDE, BLOCK), f32),
            pltpu.VMEM((2 * MIGH * 3 * STRIDE, BLOCK), f32),
            pltpu.VMEM((16, DEPTH), f32),
            pltpu.VMEM((16 * requests, BLOCK), f32),
            pltpu.VMEM((DEPTH, DEPTH), bf16),
            pltpu.VMEM((3 * DEPTH, DEPTH), bf16),
            pltpu.VMEM((2 * DEPTH, DEPTH), bf16),
            pltpu.VMEM((PIX, 3 * DEPTH), bf16),
            pltpu.VMEM((PIX, DEPTH), f32),
            pltpu.VMEM((PIX, DEPTH), f32),
            pltpu.VMEM((PIX, DEPTH), bf16),
            pltpu.VMEM((PIX, DEPTH), bf16),
            pltpu.VMEM((PIX, DEPTH), f32),
            pltpu.VMEM((PIX, 2 * DEPTH), bf16),
            pltpu.VMEM((PIX, DEPTH), f32),
            pltpu.VMEM((16 * requests, BLOCK), f32),
            dma((3, nb)),
            dma((3, nb)),
            dma((nr,)),
            dma((nr,)),
            dma((nx,)),
            dma((nx,)),
            dma(()),
            dma((2 * ITERS, nr)),
            dma((2 * ITERS, nr)),
            dma((ITERS, nx)),
            dma((ITERS, nx)),
            dma((2,)),
            dma((2,)),
        ],
        compiler_params=pltpu.CompilerParams(
            collective_id=0, has_side_effects=True, vmem_limit_bytes=48 * 1024 * 1024
        ),
        cost_estimate=pl.CostEstimate(flops=20_000_000_000, bytes_accessed=6_000_000, transcendentals=4_000_000),
        name="train",
    )(
        tile_corner.reshape(ITERS, 2 * tiles),
        own,
        migration[0],
        table,
        jnp.pad(jnp.transpose(slot).astype(f32), ((0, 0), (0, BLOCK - ITERS))),
        packed,
        depth_order.reshape(ITERS * tiles, 1, DEPTH),
        targets.reshape(ITERS * tiles, 3, PIX),
        params,
        first_moment,
        second_moment,
    )
    return new_params, new_first, new_second, pictures.reshape(ITERS, 1, tiles, 3, PIX)


def solution(mesh):
    return jax.shard_map(
        local,
        mesh=mesh,
        in_specs=(
            P(None, "row"),
            P(None, "row"),
            P(None, "row"),
            P(None, "rep", None),
            P(None, "rep", "row", None),
            P(None, "rep", "row", None),
            P(None, "rep", "row", None),
            P(None, "rep", "row", None),
            P(None, "rep", "row", None, None),
            P("row", None, None),
        ),
        out_specs=(
            P(None, "row"),
            P(None, "row"),
            P(None, "row"),
            P(None, "rep", "row", None, None),
        ),
        check_vma=False,
    )
```

```python
import functools

import jax
import jax.numpy as jnp
from jax import lax
from jax.experimental import pallas as pl
from jax.experimental.pallas import tpu as pltpu
from jax.sharding import PartitionSpec as P

P_SIZE = 59
BLOCK = 128
LISTB = 4
PIX = 256
SIDE = 16
ITERS = 2
MIGH = 2
DEPTH = 512
NINE = 9
CAP = 2
STRIDE = 72
PAIR = 24
ROUND = 40
UNROLL = 9
MESH = pl.DeviceIdType.MESH
f32 = jnp.float32
bf16 = jnp.bfloat16

harm_zero = 0.28209479177387814
harm_one = 0.4886025119029199
harm_two = (
    1.0925484305920792,
    -1.0925484305920792,
    0.31539156525252005,
    -1.0925484305920792,
    0.5462742152960396,
)
harm_three = (
    -0.5900435899266435,
    2.890611442640554,
    -0.4570457994644658,
    0.3731763325901154,
    -0.4570457994644658,
    1.445305721320277,
    -0.5900435899266435,
)
learn_rate = 0.01
adam_epsilon = 1e-08


def harmonics(face_x, face_y, face_z):
    face_xx, face_yy, face_zz = (face_x * face_x, face_y * face_y, face_z * face_z)
    return [
        harm_zero + 0.0 * face_x,
        -harm_one * face_y,
        harm_one * face_z,
        -harm_one * face_x,
        harm_two[0] * face_x * face_y,
        harm_two[1] * face_y * face_z,
        harm_two[2] * (2.0 * face_zz - face_xx - face_yy),
        harm_two[3] * face_x * face_z,
        harm_two[4] * (face_xx - face_yy),
        harm_three[0] * face_y * (3.0 * face_xx - face_yy),
        harm_three[1] * face_x * face_y * face_z,
        harm_three[2] * face_y * (4.0 * face_zz - face_xx - face_yy),
        harm_three[3] * face_z * (2.0 * face_zz - 3.0 * face_xx - 3.0 * face_yy),
        harm_three[4] * face_x * (4.0 * face_zz - face_xx - face_yy),
        harm_three[5] * face_z * (face_xx - face_yy),
        harm_three[6] * face_x * (face_xx - 3.0 * face_yy),
    ]


def split2(x):
    high = x.astype(bf16)
    return high, (x - high.astype(f32)).astype(bf16)


def split3(x):
    high = x.astype(bf16)
    rest = x - high.astype(f32)
    mid = rest.astype(bf16)
    return high, mid, (rest - mid.astype(f32)).astype(bf16)


def dot(a, b, dims=((1,), (0,))):
    return lax.dot_general(a, b, (dims, ((), ())), preferred_element_type=f32)


NT = ((1,), (1,))


def geometry(rows):
    scales = [jnp.exp(rows(3 + k)) for k in range(3)]
    q = [rows(6 + k) for k in range(4)]
    inverse = 1.0 / jnp.sqrt(q[0] * q[0] + q[1] * q[1] + q[2] * q[2] + q[3] * q[3])
    w, x, y, z = [v * inverse for v in q]
    rotation = [
        [1.0 - 2.0 * (y * y + z * z), 2.0 * (x * y - w * z), 2.0 * (x * z + w * y)],
        [2.0 * (x * y + w * z), 1.0 - 2.0 * (x * x + z * z), 2.0 * (y * z - w * x)],
        [2.0 * (x * z - w * y), 2.0 * (y * z + w * x), 1.0 - 2.0 * (x * x + y * y)],
    ]
    return scales, (w, x, y, z), inverse, rotation


def conic_of(affine, scales, rotation):
    spread = [
        [
            (affine[i][0] * rotation[0][k] + affine[i][1] * rotation[1][k] + affine[i][2] * rotation[2][k])
            * scales[k]
            for k in range(3)
        ]
        for i in range(2)
    ]
    s0, s1 = spread
    cov_xx = s0[0] * s0[0] + s0[1] * s0[1] + s0[2] * s0[2] + 0.3
    cov_yy = s1[0] * s1[0] + s1[1] * s1[1] + s1[2] * s1[2] + 0.3
    cov_xy = s0[0] * s1[0] + s0[1] * s1[1] + s0[2] * s1[2]
    over = 1.0 / (cov_xx * cov_yy - cov_xy * cov_xy)
    return spread, (cov_yy * over, -cov_xy * over, cov_xx * over)


def sigmoid(x):
    return 1.0 / (1.0 + jnp.exp(-x))


def kernel(
    nr,
    nx,
    nb,
    tiles,
    corner_ref,
    own_ref,
    migration_ref,
    request_ref,
    column_ref,
    camera_ref,
    order_ref,
    target_ref,
    p_hbm,
    m_hbm,
    v_hbm,
    p_out,
    m_out,
    v_out,
    picture_ref,
    p_s,
    m_s,
    v_s,
    ask_send,
    ask_recv,
    cam_recv,
    cam_smem,
    f_send,
    f_recv,
    g_send,
    g_recv,
    shared,
    mig_send,
    mig_recv,
    end_send,
    end_recv,
    listing,
    listed_rows,
    picks,
    upper,
    lower,
    logs,
    alphas,
    passing,
    weight_high,
    weight_low,
    pulls,
    products,
    behind,
    request_grads,
    local_sem,
    out_sem,
    ask_ssem,
    ask_rsem,
    cam_ssem,
    cam_rsem,
    cam_sem,
    a2a_ssem,
    a2a_rsem,
    rep_ssem,
    rep_rsem,
    mig_ssem,
    mig_rsem,
    end_ssem,
    end_rsem,
):
    me = lax.axis_index("row")
    rep = lax.axis_index("rep")
    state = (p_s, m_s, v_s)

    def block_rows(ref, b):
        return ref.at[pl.ds(pl.multiple_of(STRIDE * b, 8), P_SIZE), :]

    def lanes_of(ref, b):
        return ref.at[:, pl.ds(pl.multiple_of(BLOCK * b, BLOCK), BLOCK)]

    def load_copy(a, b):
        return pltpu.make_async_copy(
            lanes_of((p_hbm, m_hbm, v_hbm)[a], b), block_rows(state[a], b), local_sem.at[a, b]
        )

    for a in range(3):
        lax.fori_loop(0, nb, lambda b, c: (load_copy(a, b).start(), c)[1], 0)

    barrier = pltpu.get_barrier_semaphore()

    def greet_row(k, c):
        pl.semaphore_signal(barrier, 1, device_id={"row": lax.rem(me + k, nr)}, device_id_type=MESH)
        return c

    def greet_rep(k, c):
        pl.semaphore_signal(barrier, 1, device_id={"rep": lax.rem(rep + k, nx)}, device_id_type=MESH)
        return c

    lax.fori_loop(1, nr, greet_row, 0, unroll=UNROLL)
    lax.fori_loop(1, nx, greet_rep, 0)

    asked_now = jnp.full((nr, BLOCK), -1, jnp.int32)
    lane = lax.broadcasted_iota(jnp.int32, (nr, BLOCK), 1)
    owner_id = lax.broadcasted_iota(jnp.int32, (nr, BLOCK), 0)
    requests = tiles * LISTB
    for i in range(ITERS):
        for s in range(CAP):
            match = (owner_id * CAP + s == request_ref[i : i + 1, :]) & (lane < requests)
            column = jnp.sum(
                jnp.where(match, request_ref[ITERS + i : ITERS + i + 1, :] + 1.0, 0.0), axis=1, keepdims=True
            )
            asked_now = jnp.where(lane == CAP * i + s, column.astype(jnp.int32) - 1, asked_now)
    ask_send[pl.ds(0, nr, stride=8), :] = asked_now
    cam_recv[pl.ds(pl.multiple_of(8 * rep, 8), 1), :] = camera_ref[...]

    pl.semaphore_wait(barrier, nr + nx - 2)

    def row_of(k):
        return lax.rem(me + k, nr), lax.rem(me + nr - k, nr)

    def ask_copy(k, at):
        to, _ = row_of(k)
        return pltpu.make_async_remote_copy(
            src_ref=ask_send.at[pl.ds(pl.multiple_of(8 * to, 8), 1), :],
            dst_ref=ask_recv.at[pl.ds(pl.multiple_of(8 * at, 8), 1), :],
            send_sem=ask_ssem.at[k],
            recv_sem=ask_rsem.at[k],
            device_id={"row": to},
            device_id_type=MESH,
        )

    def cam_copy(k, at):
        return pltpu.make_async_remote_copy(
            src_ref=cam_recv.at[pl.ds(pl.multiple_of(8 * rep, 8), 1), :],
            dst_ref=cam_recv.at[pl.ds(pl.multiple_of(8 * at, 8), 1), :],
            send_sem=cam_ssem.at[k],
            recv_sem=cam_rsem.at[k],
            device_id={"rep": lax.rem(rep + k, nx)},
            device_id_type=MESH,
        )

    lax.fori_loop(1, nr, lambda k, c: (ask_copy(k, me).start(), c)[1], 0)
    for k in range(1, nx):
        cam_copy(k, rep).start()
    own_ask = pl.ds(pl.multiple_of(8 * me, 8), 8)
    ask_recv[own_ask, :] = ask_send[own_ask, :]

    square = lax.broadcasted_iota(jnp.int32, (DEPTH, DEPTH), 0), lax.broadcasted_iota(jnp.int32, (DEPTH, DEPTH), 1)
    before = jnp.where(square[0] < square[1], 1.0, 0.0).astype(bf16)
    after = jnp.where(square[0] > square[1], 1.0, 0.0).astype(bf16)
    for part in range(3):
        upper[part * DEPTH : (part + 1) * DEPTH, :] = before
    for part in range(2):
        lower[part * DEPTH : (part + 1) * DEPTH, :] = after
    listed_rows[...] = jnp.zeros_like(listed_rows)
    request_grads[...] = jnp.zeros_like(request_grads)

    for a in range(3):
        lax.fori_loop(0, nb, lambda b, c: (load_copy(a, b).wait(), c)[1], 0)

    def row(ref, r):
        return ref[pl.ds(r, nb, stride=STRIDE), :]

    def put_row(ref, r, x):
        ref[pl.ds(r, nb, stride=STRIDE), :] = x

    def project(i):
        cam = [own_ref[i, 0, k] for k in range(11)]
        affine = [cam[0:3], cam[3:6]]
        rows = functools.partial(row, p_s)
        scales, _, _, rotation = geometry(rows)
        _, conic = conic_of(affine, scales, rotation)
        means = [rows(k) for k in range(3)]
        centre = [
            affine[j][0] * means[0] + affine[j][1] * means[1] + affine[j][2] * means[2] + cam[6 + j] for j in range(2)
        ]
        basis = harmonics(*cam[8:11])
        colours = []
        for k in range(3):
            total = basis[0] * rows(11 + k)
            for j in range(1, 16):
                total = total + basis[j] * rows(11 + 3 * j + k)
            colours.append(0.5 + total)
        return centre + list(conic) + colours + [sigmoid(rows(10))]

    def put_slot(ref, values):
        for c in range(NINE):
            ref[pl.ds(c, nr, stride=PAIR), :] = values[:, c * BLOCK : (c + 1) * BLOCK]

    def get_slot(ref, components=range(NINE)):
        return jnp.concatenate([ref[pl.ds(c, nr, stride=PAIR), :] for c in components], axis=1)

    def nine_rows(p):
        return pl.ds(pl.multiple_of(PAIR * p, 8), NINE)

    def slot_copy(send, recv, which, s, k, at):
        to, _ = row_of(k)
        return pltpu.make_async_remote_copy(
            src_ref=send.at[s, nine_rows(to), :],
            dst_ref=recv.at[s, nine_rows(at), :],
            send_sem=a2a_ssem.at[CAP * which + s, k],
            recv_sem=a2a_rsem.at[CAP * which + s, k],
            device_id={"row": to},
            device_id_type=MESH,
        )

    def slot_start(send, recv, which, s):
        lax.fori_loop(
            1, nr, lambda k, c: (slot_copy(send, recv, which, s, k, me).start(), c)[1], 0, unroll=UNROLL
        )
        recv[s, nine_rows(me), :] = send[s, nine_rows(me), :]

    def slot_arrive(send, recv, which, s):
        lax.fori_loop(
            1,
            nr,
            lambda k, c: (slot_copy(send, recv, which, s, k, row_of(k)[1]).wait_recv(), c)[1],
            0,
            unroll=UNROLL,
        )

    def slot_leave(send, recv, which):
        for s in range(CAP):
            lax.fori_loop(
                1, nr, lambda k, c: (slot_copy(send, recv, which, s, k, me).wait_send(), c)[1], 0, unroll=UNROLL
            )

    def render(i, f_out, f_in, g_out, g_in):
        def list_slot(s):
            slot_lane = CAP * lax.broadcasted_iota(jnp.int32, (requests, nr), 1) + s
            take = jnp.where(column_ref[:, i : i + 1] == slot_lane.astype(f32), 1.0, 0.0).astype(bf16)
            slot_arrive(f_out, f_in, 2 * i, s)
            pieces = split3(get_slot(f_in.at[s]))
            listed = dot(take, pieces[0]) + dot(take, pieces[1]) + dot(take, pieces[2])
            for c in range(NINE):
                at = pl.ds(c, requests, stride=16)
                fresh = listed[:, BLOCK * c : BLOCK * (c + 1)]
                listed_rows[at, :] = fresh if s == 0 else listed_rows[at, :] + fresh

        def return_slot(s):
            by_request = jnp.concatenate(
                [request_grads[pl.ds(c, requests, stride=16), :] for c in range(NINE)], axis=1
            )
            slot_line = CAP * lax.broadcasted_iota(jnp.int32, (nr, 3 * requests), 0) + s
            back = jnp.where(slot_line.astype(f32) == request_ref[i : i + 1, 0 : 3 * requests], 1.0, 0.0).astype(bf16)
            put_slot(g_out.at[s], dot(back, jnp.concatenate(split3(by_request), axis=0)))
            slot_start(g_out, g_in, 2 * i + 1, s)

        list_slot(0)

        def one_tile(t, carry):
            @pl.when(t == 1)
            def _():
                list_slot(1)

            @pl.when(t == tiles - 1)
            def _():
                return_slot(0)

            for j in range(LISTB):
                listing[:, BLOCK * j : BLOCK * (j + 1)] = listed_rows[
                    pl.ds(pl.multiple_of(16 * (LISTB * t + j), 16), 16), :
                ]
            order = order_ref[i, 0, pl.ds(t, 1), :]
            pick = jnp.where(lax.broadcasted_iota(jnp.int32, (DEPTH, DEPTH), 0) == order, 1.0, 0.0).astype(bf16)
            picks[...] = pick
            parts = dot(jnp.concatenate(split3(listing[...]), axis=0), picks[...])
            splats = parts[0:16] + parts[16:32] + parts[32:48]
            centre_x, centre_y = splats[0:1], splats[1:2]
            conic_a, conic_b, conic_c = splats[2:3], splats[3:4], splats[4:5]
            opacity = splats[8:9]
            ticks = lax.broadcasted_iota(jnp.int32, (SIDE, DEPTH), 0).astype(f32)
            gap_x = (corner_ref[i, 0, t, 0] + ticks + 0.5) - centre_x
            gap_y = (corner_ref[i, 0, t, 1] + ticks + 0.5) - centre_y
            along = -0.5 * conic_a * gap_x * gap_x
            cross = -conic_b * gap_y
            across = -0.5 * conic_c * gap_y * gap_y
            for y in range(SIDE):
                at = slice(SIDE * y, SIDE * (y + 1))
                alpha = opacity * jnp.exp(along + across[y : y + 1] + gap_x * cross[y : y + 1])
                alphas[at, :] = alpha
                for part, piece in enumerate(split3(jnp.log(1.0 - alpha))):
                    logs[at, part * DEPTH : (part + 1) * DEPTH] = piece
            passing[...] = dot(logs[...], upper[...])
            for y in range(SIDE):
                at = slice(SIDE * y, SIDE * (y + 1))
                through = jnp.exp(passing[at, :])
                passing[at, :] = through
                high, low = split2(alphas[at, :] * through)
                weight_high[at, :] = high
                weight_low[at, :] = low
            eight = lax.broadcasted_iota(jnp.int32, (8, 1), 0)
            paint = jnp.where(eight >= 5, splats[0:8], 0.0)
            paint_high = paint.astype(bf16).astype(f32)
            paint_low = paint - paint_high
            both = dot(jnp.concatenate([paint_high, paint_low], axis=0).astype(bf16), weight_high[...], NT)
            high_low = dot(jnp.concatenate([paint_high, paint_high], axis=0).astype(bf16), weight_low[...], NT)
            picture = both[0:8] + both[8:16] + high_low[0:8]
            picture_ref[i, 0, t] = picture[5:8]
            residual = picture - jnp.concatenate([jnp.zeros((5, PIX), f32), target_ref[i, 0, t]], axis=0)
            res_high = residual.astype(bf16).astype(f32)
            res_low = residual - res_high
            pull = dot(
                jnp.transpose(jnp.concatenate([res_high, res_high, res_low, res_low], axis=0)).astype(bf16),
                jnp.concatenate([paint_high, paint_low, paint_high, paint_low], axis=0).astype(bf16),
            )
            pulls[...] = pull
            both = dot(jnp.concatenate([res_high, res_low], axis=0).astype(bf16), weight_high[...])
            high_low = dot(jnp.concatenate([res_high, res_high], axis=0).astype(bf16), weight_low[...])
            colour_grads = both[0:8] + both[8:16] + high_low[0:8]
            for y in range(SIDE):
                at = slice(SIDE * y, SIDE * (y + 1))
                for part, piece in enumerate(split2(alphas[at, :] * passing[at, :] * pulls[at, :])):
                    products[at, part * DEPTH : (part + 1) * DEPTH] = piece
            behind[...] = dot(products[...], lower[...])
            sums = [jnp.zeros((SIDE, DEPTH), f32) for _ in range(3)]
            for y in range(SIDE):
                at = slice(SIDE * y, SIDE * (y + 1))
                alpha = alphas[at, :]
                felt = alpha * (passing[at, :] * pulls[at, :] - behind[at, :] / (1.0 - alpha))
                tall = felt * gap_y[y : y + 1]
                sums = [sums[0] + felt, sums[1] + tall, sums[2] + tall * gap_y[y : y + 1]]

            def over_x(v):
                return jnp.sum(v, axis=0, keepdims=True)

            felt_x = gap_x * sums[0]
            total, total_x, total_xx = over_x(sums[0]), over_x(felt_x), over_x(gap_x * felt_x)
            total_y, total_xy, total_yy = over_x(sums[1]), over_x(gap_x * sums[1]), over_x(sums[2])
            grads = jnp.concatenate(
                [
                    conic_a * total_x + conic_b * total_y,
                    conic_b * total_x + conic_c * total_y,
                    -0.5 * total_xx,
                    -total_xy,
                    -0.5 * total_yy,
                    colour_grads[5:8],
                    total / opacity,
                    jnp.zeros((7, DEPTH), f32),
                ],
                axis=0,
            )
            parts = dot(jnp.concatenate(split3(grads), axis=0), picks[...], NT)
            listed = parts[0:16] + parts[16:32] + parts[32:48]
            for j in range(LISTB):
                request_grads[pl.ds(pl.multiple_of(16 * (LISTB * t + j), 16), 16), :] = listed[
                    :, BLOCK * j : BLOCK * (j + 1)
                ]
            return carry

        lax.fori_loop(0, tiles, one_tile, 0)
        return_slot(1)

    def own_get(a, r):
        return row(state[a], r)

    def own_put(a, r, x):
        put_row(state[a], r, x)

    def step_up(get, put, r, gradient):
        one = 0.9 * get(1, r) + 0.1 * gradient
        two = 0.999 * get(2, r) + 0.001 * gradient * gradient
        put(1, r, one)
        put(2, r, two)
        put(0, r, get(0, r) - learn_rate * one / (jnp.sqrt(two) + adam_epsilon))

    def cameras(i):
        return [[cam_smem[8 * x, 11 * i + k] for k in range(11)] for x in range(nx)]

    def pull_colours(i, get, put, share):
        opacity = sigmoid(get(0, 10))
        fades = share(0, 8)
        for x in range(1, nx):
            fades = fades + share(x, 8)
        step_up(get, put, 10, fades * opacity * (1.0 - opacity))
        bases = [harmonics(*cam[8:11]) for cam in cameras(i)]
        for k in range(3):
            felt = [share(x, 5 + k) for x in range(nx)]
            for j in range(16):
                total = bases[0][j] * felt[0]
                for x in range(1, nx):
                    total = total + bases[x][j] * felt[x]
                step_up(get, put, 11 + 3 * j + k, total)

    def pull_shapes(i, get, put, share):
        scales, quats, inverse, rotation = geometry(lambda r: get(0, r))
        turn = None
        for x, cam in enumerate(cameras(i)):
            affine = [cam[0:3], cam[3:6]]
            spread, (con_a, con_b, con_c) = conic_of(affine, scales, rotation)
            g_a, g_b, g_c = share(x, 2), 0.5 * share(x, 3), share(x, 4)
            left_a, left_b = g_a * con_a + g_b * con_b, g_a * con_b + g_b * con_c
            right_a, right_b = g_b * con_a + g_c * con_b, g_b * con_b + g_c * con_c
            n_xx = -2.0 * (con_a * left_a + con_b * right_a)
            n_xy = -2.0 * (con_a * left_b + con_b * right_b)
            n_yy = -2.0 * (con_b * left_b + con_c * right_b)
            felt = [
                [n_xx * spread[0][k] + n_xy * spread[1][k] for k in range(3)],
                [n_xy * spread[0][k] + n_yy * spread[1][k] for k in range(3)],
            ]
            stretch = [felt[0][k] * spread[0][k] + felt[1][k] * spread[1][k] for k in range(3)]
            twist = [
                [(affine[0][j] * felt[0][k] + affine[1][j] * felt[1][k]) * scales[k] for k in range(3)]
                for j in range(3)
            ]
            moved = [affine[0][j] * share(x, 0) + affine[1][j] * share(x, 1) for j in range(3)]
            if turn is None:
                stretches, turn, moves = stretch, twist, moved
            else:
                stretches = [u + v for u, v in zip(stretches, stretch)]
                turn = [[u + v for u, v in zip(a, b)] for a, b in zip(turn, twist)]
                moves = [u + v for u, v in zip(moves, moved)]
        w, x, y, z = quats
        d = turn
        unit = [
            2.0 * (z * (d[1][0] - d[0][1]) + y * (d[0][2] - d[2][0]) + x * (d[2][1] - d[1][2])),
            2.0
            * (
                y * (d[0][1] + d[1][0])
                + z * (d[0][2] + d[2][0])
                + w * (d[2][1] - d[1][2])
                - 2.0 * x * (d[1][1] + d[2][2])
            ),
            2.0
            * (
                x * (d[0][1] + d[1][0])
                + w * (d[0][2] - d[2][0])
                + z * (d[1][2] + d[2][1])
                - 2.0 * y * (d[0][0] + d[2][2])
            ),
            2.0
            * (
                w * (d[1][0] - d[0][1])
                + x * (d[0][2] + d[2][0])
                + y * (d[1][2] + d[2][1])
                - 2.0 * z * (d[0][0] + d[1][1])
            ),
        ]
        inner = unit[0] * w + unit[1] * x + unit[2] * y + unit[3] * z
        for k in range(3):
            step_up(get, put, k, moves[k])
        for k in range(3):
            step_up(get, put, 3 + k, stretches[k])
        for k in range(4):
            step_up(get, put, 6 + k, (unit[k] - quats[k] * inner) * inverse)

    parts_of = ((5, 4), (0, 5))

    def share_copy(i, part, k, at):
        first, count = parts_of[part]

        def rows_at(x):
            return pl.ds(pl.multiple_of((NINE * x + first) * nb, 8), count * nb)

        return pltpu.make_async_remote_copy(
            src_ref=shared.at[i, rows_at(rep), :],
            dst_ref=shared.at[i, rows_at(at), :],
            send_sem=rep_ssem.at[2 * i + part, k],
            recv_sem=rep_rsem.at[2 * i + part, k],
            device_id={"rep": lax.rem(rep + k, nx)},
            device_id_type=MESH,
        )

    hand = MIGH * 3 * STRIDE
    round_rows = MIGH * ROUND

    def neighbour(side):
        return {"row": lax.rem(me + (nr - 1 if side == 0 else 1), nr)}

    def hand_copy(side):
        return pltpu.make_async_remote_copy(
            src_ref=mig_send.at[pl.ds(side * hand, hand), :],
            dst_ref=mig_recv.at[pl.ds((1 - side) * hand, hand), :],
            send_sem=mig_ssem.at[side],
            recv_sem=mig_rsem.at[side],
            device_id=neighbour(side),
            device_id_type=MESH,
        )

    def end_copy(side):
        return pltpu.make_async_remote_copy(
            src_ref=end_send.at[pl.ds(side * round_rows, round_rows), :],
            dst_ref=end_recv.at[pl.ds((1 - side) * round_rows, round_rows), :],
            send_sem=end_ssem.at[side],
            recv_sem=end_rsem.at[side],
            device_id=neighbour(side),
            device_id_type=MESH,
        )

    def hand_over():
        for side in range(2):
            for j in range(MIGH):
                leaving = jnp.full((STRIDE, BLOCK), migration_ref[0, side, j], jnp.int32)
                for a in range(3):
                    at = side * hand + (3 * j + a) * STRIDE
                    chosen = state[a][0:STRIDE, :]
                    for b in range(1, nb):
                        chosen = jnp.where(leaving == b, state[a][STRIDE * b : STRIDE * (b + 1), :], chosen)
                    mig_send[at : at + STRIDE, :] = chosen
            hand_copy(side).start()

    def hand_gradients(share):
        count = 2 * MIGH
        line = lax.broadcasted_iota(jnp.int32, (8, 3 * nb), 0)
        block_lane = lax.rem(lax.broadcasted_iota(jnp.int32, (8, 3 * nb), 1), nb)
        mine = jnp.full((8, 3 * nb), -1, jnp.int32)
        for side in range(2):
            for j in range(MIGH):
                mine = jnp.where(line == MIGH * side + j, migration_ref[0, side, j], mine)
        choose = jnp.where(mine == block_lane, 1.0, 0.0)
        choose = jnp.concatenate([choose, jnp.zeros_like(choose)], axis=0).astype(bf16)
        for x in range(nx):
            values = jnp.concatenate([share(x, c) for c in range(NINE)], axis=1)
            chosen = dot(choose, jnp.concatenate(split3(values), axis=0))
            for c in range(NINE):
                end_send[pl.ds(NINE * x + c, count, stride=ROUND), :] = chosen[0:count, BLOCK * c : BLOCK * (c + 1)]
        for side in range(2):
            end_copy(side).start()

    asked_columns = asked_lines = None
    for i in range(ITERS):
        projected = jnp.concatenate(project(i), axis=1)
        if i == 0:

            def asked(k, c):
                copy = ask_copy(k, row_of(k)[1])
                copy.wait_recv()
                copy.wait_send()
                return c

            lax.fori_loop(1, nr, asked, 0)
            asked_all = ask_recv[pl.ds(0, nr, stride=8), :].astype(f32)
            asked_columns = asked_all
            asked_lines = jnp.transpose(
                asked_all
                if nr == BLOCK
                else jnp.concatenate([asked_all, jnp.zeros((BLOCK - nr, BLOCK), f32)], axis=0)
            )
        block_lane = lax.rem(lax.broadcasted_iota(jnp.int32, (nr, 3 * nb), 1), nb).astype(f32)
        serve = jnp.concatenate(
            [
                jnp.where(asked_columns[:, CAP * i + s : CAP * i + s + 1] == block_lane, 1.0, 0.0)
                for s in range(CAP)
            ],
            axis=0,
        ).astype(bf16)
        slots = jnp.concatenate(split3(projected), axis=0)
        for s in range(CAP):
            put_slot(f_send.at[i, s], dot(serve[s * nr : (s + 1) * nr], slots))
            slot_start(f_send.at[i], f_recv.at[i], 2 * i, s)
        render(i, f_send.at[i], f_recv.at[i], g_send.at[i], g_recv.at[i])
        slot_leave(f_send.at[i], f_recv.at[i], 2 * i)
        block_line = lax.broadcasted_iota(jnp.int32, (nb, nr), 0).astype(f32)
        gathers = [
            jnp.where(block_line == asked_lines[CAP * i + s : CAP * i + s + 1, 0:nr], 1.0, 0.0).astype(bf16)
            for s in range(CAP)
        ]

        def sum_slot(s, first, count):
            pieces = split3(get_slot(g_recv.at[i, s], range(first, first + count)))
            return dot(gathers[s], pieces[0]) + dot(gathers[s], pieces[1]) + dot(gathers[s], pieces[2])

        slot_arrive(g_send.at[i], g_recv.at[i], 2 * i + 1, 0)
        sums = [sum_slot(0, *parts_of[part]) for part in range(2)]
        slot_arrive(g_send.at[i], g_recv.at[i], 2 * i + 1, 1)
        for part in range(2):
            first, count = parts_of[part]
            summed = sums[part] + sum_slot(1, first, count)
            for c in range(count):
                shared[i, pl.ds(pl.multiple_of((NINE * rep + first + c) * nb, 8), nb), :] = summed[
                    :, BLOCK * c : BLOCK * (c + 1)
                ]
            for k in range(1, nx):
                share_copy(i, part, k, rep).start()
        slot_leave(g_send.at[i], g_recv.at[i], 2 * i + 1)
        if i == 0:
            for k in range(1, nx):
                copy = cam_copy(k, lax.rem(rep + nx - k, nx))
                copy.wait_recv()
                copy.wait_send()
            table = pltpu.make_async_copy(cam_recv, cam_smem, cam_sem)
            table.start()
            table.wait()

        def own_share(x, c):
            at = (x * NINE + c) * nb
            return shared[i, at : at + nb, :]

        def arrive_share(part):
            for k in range(1, nx):
                copy = share_copy(i, part, k, lax.rem(rep + nx - k, nx))
                copy.wait_recv()
                copy.wait_send()

        arrive_share(0)
        pull_colours(i, own_get, own_put, own_share)
        arrive_share(1)
        if i == ITERS - 1:
            hand_gradients(own_share)
        pull_shapes(i, own_get, own_put, own_share)
        if i == ITERS - 2:
            hand_over()

    for side in range(2):
        hand_copy(side).wait_recv()
        hand_copy(side).wait_send()
        end_copy(side).wait_recv()
        end_copy(side).wait_send()

    def come_get(a, r):
        return mig_recv[pl.ds(a * STRIDE + r, 2 * MIGH, stride=3 * STRIDE), :]

    def come_put(a, r, x):
        mig_recv[pl.ds(a * STRIDE + r, 2 * MIGH, stride=3 * STRIDE), :] = x

    def come_share(x, c):
        return end_recv[pl.ds(NINE * x + c, 2 * MIGH, stride=ROUND), :]

    pull_colours(ITERS - 1, come_get, come_put, come_share)
    pull_shapes(ITERS - 1, come_get, come_put, come_share)

    def settle(b, carry):
        for a in range(3):
            at = pl.ds(pl.multiple_of(STRIDE * b, STRIDE), STRIDE)
            block = state[a][at, :]
            for side in range(2):
                for j in range(MIGH):
                    source = side * hand + (3 * j + a) * STRIDE
                    here = jnp.full((STRIDE, BLOCK), migration_ref[0, side, j], jnp.int32) == b
                    block = jnp.where(here, mig_recv[source : source + STRIDE, :], block)
            state[a][at, :] = block
            store_copy(a, b).start()
        return carry

    def store_copy(a, b):
        return pltpu.make_async_copy(
            block_rows(state[a], b), lanes_of((p_out, m_out, v_out)[a], b), out_sem.at[a, b]
        )

    lax.fori_loop(0, nb, settle, 0)
    for a in range(3):
        lax.fori_loop(0, nb, lambda b, c: (store_copy(a, b).wait(), c)[1], 0)


def local(
    params,
    first_moment,
    second_moment,
    camera,
    tile_corner,
    tile_owner,
    tile_block,
    depth_order,
    targets,
    migration,
):
    nr, nx = lax.axis_size("row"), lax.axis_size("rep")
    local_gauss = params.shape[1]
    nb = local_gauss // BLOCK
    tiles = tile_owner.shape[2]
    requests = tiles * LISTB
    owner = tile_owner.reshape(ITERS, requests)
    block = tile_block.reshape(ITERS, requests)
    position = jnp.arange(requests, dtype=jnp.int32)
    same = (owner[:, :, None] == owner[:, None, :]) & (position[None, :] < position[:, None])
    later = jnp.any(same, axis=2) | (position >= requests - LISTB)[None, :]
    slot = owner * CAP + later.astype(jnp.int32)
    wide = jnp.concatenate([slot, slot, slot], axis=1).astype(f32)
    table = jnp.concatenate(
        [
            jnp.pad(wide, ((0, 0), (0, BLOCK - 3 * requests)), constant_values=-1.0),
            jnp.pad(block.astype(f32), ((0, 0), (0, BLOCK - requests))),
            jnp.zeros((8 - 2 * ITERS, BLOCK), f32),
        ],
        axis=0,
    )
    own = camera.reshape(ITERS, 11)
    packed = jnp.pad(own.reshape(1, ITERS * 11), ((0, 0), (0, BLOCK - ITERS * 11)))

    vmem = pl.BlockSpec(memory_space=pltpu.VMEM)
    smem = pl.BlockSpec(memory_space=pltpu.SMEM)
    hbm = pl.BlockSpec(memory_space=pl.ANY)
    size = jax.ShapeDtypeStruct((P_SIZE, local_gauss), f32)
    dma = pltpu.SemaphoreType.DMA
    new_params, new_first, new_second, pictures = pl.pallas_call(
        functools.partial(kernel, nr, nx, nb, tiles),
        out_shape=(size, size, size, jax.ShapeDtypeStruct((ITERS, 1, tiles, 3, PIX), f32)),
        in_specs=[smem] * 3 + [vmem] * 5 + [hbm] * 3,
        out_specs=(hbm, hbm, hbm, vmem),
        scratch_shapes=[
            pltpu.VMEM((STRIDE * nb, BLOCK), f32),
            pltpu.VMEM((STRIDE * nb, BLOCK), f32),
            pltpu.VMEM((STRIDE * nb, BLOCK), f32),
            pltpu.VMEM((8 * nr, BLOCK), jnp.int32),
            pltpu.VMEM((8 * nr, BLOCK), jnp.int32),
            pltpu.VMEM((8 * nx, BLOCK), f32),
            pltpu.SMEM((8 * nx, BLOCK), f32),
            pltpu.VMEM((ITERS, CAP, PAIR * nr, BLOCK), f32),
            pltpu.VMEM((ITERS, CAP, PAIR * nr, BLOCK), f32),
            pltpu.VMEM((ITERS, CAP, PAIR * nr, BLOCK), f32),
            pltpu.VMEM((ITERS, CAP, PAIR * nr, BLOCK), f32),
            pltpu.VMEM((ITERS, nx * NINE * nb, BLOCK), f32),
            pltpu.VMEM((2 * MIGH * 3 * STRIDE, BLOCK), f32),
            pltpu.VMEM((2 * MIGH * 3 * STRIDE, BLOCK), f32),
            pltpu.VMEM((2 * MIGH * ROUND, BLOCK), f32),
            pltpu.VMEM((2 * MIGH * ROUND, BLOCK), f32),
            pltpu.VMEM((16, DEPTH), f32),
            pltpu.VMEM((16 * requests, BLOCK), f32),
            pltpu.VMEM((DEPTH, DEPTH), bf16),
            pltpu.VMEM((3 * DEPTH, DEPTH), bf16),
            pltpu.VMEM((2 * DEPTH, DEPTH), bf16),
            pltpu.VMEM((PIX, 3 * DEPTH), bf16),
            pltpu.VMEM((PIX, DEPTH), f32),
            pltpu.VMEM((PIX, DEPTH), f32),
            pltpu.VMEM((PIX, DEPTH), bf16),
            pltpu.VMEM((PIX, DEPTH), bf16),
            pltpu.VMEM((PIX, DEPTH), f32),
            pltpu.VMEM((PIX, 2 * DEPTH), bf16),
            pltpu.VMEM((PIX, DEPTH), f32),
            pltpu.VMEM((16 * requests, BLOCK), f32),
            dma((3, nb)),
            dma((3, nb)),
            dma((nr,)),
            dma((nr,)),
            dma((nx,)),
            dma((nx,)),
            dma(()),
            dma((2 * ITERS * CAP, nr)),
            dma((2 * ITERS * CAP, nr)),
            dma((2 * ITERS, nx)),
            dma((2 * ITERS, nx)),
            dma((2,)),
            dma((2,)),
            dma((2,)),
            dma((2,)),
        ],
        compiler_params=pltpu.CompilerParams(
            collective_id=0, has_side_effects=True, vmem_limit_bytes=48 * 1024 * 1024
        ),
        cost_estimate=pl.CostEstimate(flops=20_000_000_000, bytes_accessed=6_000_000, transcendentals=4_000_000),
        name="train",
    )(
        tile_corner,
        camera,
        migration,
        table,
        jnp.pad(jnp.transpose(slot).astype(f32), ((0, 0), (0, BLOCK - ITERS))),
        packed,
        depth_order,
        targets,
        params,
        first_moment,
        second_moment,
    )
    return new_params, new_first, new_second, pictures


def solution(mesh):
    return jax.shard_map(
        local,
        mesh=mesh,
        in_specs=(
            P(None, "row"),
            P(None, "row"),
            P(None, "row"),
            P(None, "rep", None),
            P(None, "rep", "row", None),
            P(None, "rep", "row", None),
            P(None, "rep", "row", None),
            P(None, "rep", "row", None),
            P(None, "rep", "row", None, None),
            P("row", None, None),
        ),
        out_specs=(
            P(None, "row"),
            P(None, "row"),
            P(None, "row"),
            P(None, "rep", "row", None, None),
        ),
        check_vma=False,
    )
```

```python
import functools

import jax
import jax.numpy as jnp
from jax import lax
from jax.experimental import pallas as pl
from jax.experimental.pallas import tpu as pltpu
from jax.sharding import PartitionSpec as P

P_SIZE = 59
BLOCK = 128
LISTB = 4
PIX = 256
SIDE = 16
ITERS = 2
MIGH = 2
DEPTH = 512
NINE = 9
CAP = 2
STRIDE = 72
PAIR = 24
ROUND = 40
UNROLL = 9
MESH = pl.DeviceIdType.MESH
f32 = jnp.float32
bf16 = jnp.bfloat16

harm_zero = 0.28209479177387814
harm_one = 0.4886025119029199
harm_two = (
    1.0925484305920792,
    -1.0925484305920792,
    0.31539156525252005,
    -1.0925484305920792,
    0.5462742152960396,
)
harm_three = (
    -0.5900435899266435,
    2.890611442640554,
    -0.4570457994644658,
    0.3731763325901154,
    -0.4570457994644658,
    1.445305721320277,
    -0.5900435899266435,
)
learn_rate = 0.01
adam_epsilon = 1e-08


def harmonics(face_x, face_y, face_z):
    face_xx, face_yy, face_zz = (face_x * face_x, face_y * face_y, face_z * face_z)
    return [
        harm_zero + 0.0 * face_x,
        -harm_one * face_y,
        harm_one * face_z,
        -harm_one * face_x,
        harm_two[0] * face_x * face_y,
        harm_two[1] * face_y * face_z,
        harm_two[2] * (2.0 * face_zz - face_xx - face_yy),
        harm_two[3] * face_x * face_z,
        harm_two[4] * (face_xx - face_yy),
        harm_three[0] * face_y * (3.0 * face_xx - face_yy),
        harm_three[1] * face_x * face_y * face_z,
        harm_three[2] * face_y * (4.0 * face_zz - face_xx - face_yy),
        harm_three[3] * face_z * (2.0 * face_zz - 3.0 * face_xx - 3.0 * face_yy),
        harm_three[4] * face_x * (4.0 * face_zz - face_xx - face_yy),
        harm_three[5] * face_z * (face_xx - face_yy),
        harm_three[6] * face_x * (face_xx - 3.0 * face_yy),
    ]


def split2(x):
    high = x.astype(bf16)
    return high, (x - high.astype(f32)).astype(bf16)


def split3(x):
    high = x.astype(bf16)
    rest = x - high.astype(f32)
    mid = rest.astype(bf16)
    return high, mid, (rest - mid.astype(f32)).astype(bf16)


def dot(a, b, dims=((1,), (0,))):
    return lax.dot_general(a, b, (dims, ((), ())), preferred_element_type=f32)


NT = ((1,), (1,))


def geometry(rows):
    scales = [jnp.exp(rows(3 + k)) for k in range(3)]
    q = [rows(6 + k) for k in range(4)]
    inverse = 1.0 / jnp.sqrt(q[0] * q[0] + q[1] * q[1] + q[2] * q[2] + q[3] * q[3])
    w, x, y, z = [v * inverse for v in q]
    rotation = [
        [1.0 - 2.0 * (y * y + z * z), 2.0 * (x * y - w * z), 2.0 * (x * z + w * y)],
        [2.0 * (x * y + w * z), 1.0 - 2.0 * (x * x + z * z), 2.0 * (y * z - w * x)],
        [2.0 * (x * z - w * y), 2.0 * (y * z + w * x), 1.0 - 2.0 * (x * x + y * y)],
    ]
    return scales, (w, x, y, z), inverse, rotation


def conic_of(affine, scales, rotation):
    spread = [
        [
            (affine[i][0] * rotation[0][k] + affine[i][1] * rotation[1][k] + affine[i][2] * rotation[2][k])
            * scales[k]
            for k in range(3)
        ]
        for i in range(2)
    ]
    s0, s1 = spread
    cov_xx = s0[0] * s0[0] + s0[1] * s0[1] + s0[2] * s0[2] + 0.3
    cov_yy = s1[0] * s1[0] + s1[1] * s1[1] + s1[2] * s1[2] + 0.3
    cov_xy = s0[0] * s1[0] + s0[1] * s1[1] + s0[2] * s1[2]
    over = 1.0 / (cov_xx * cov_yy - cov_xy * cov_xy)
    return spread, (cov_yy * over, -cov_xy * over, cov_xx * over)


def sigmoid(x):
    return 1.0 / (1.0 + jnp.exp(-x))


def kernel(
    nr,
    nx,
    nb,
    tiles,
    corner_ref,
    own_ref,
    migration_ref,
    request_ref,
    order_ref,
    target_ref,
    p_hbm,
    m_hbm,
    v_hbm,
    p_out,
    m_out,
    v_out,
    picture_ref,
    p_s,
    m_s,
    v_s,
    ask_send,
    ask_recv,
    cam_recv,
    cam_smem,
    f_send,
    f_recv,
    g_send,
    g_recv,
    shared,
    mig_send,
    mig_recv,
    end_send,
    end_recv,
    listing,
    listed_rows,
    picks,
    upper,
    lower,
    logs,
    alphas,
    passing,
    weight_high,
    weight_low,
    pulls,
    products,
    behind,
    request_grads,
    local_sem,
    out_sem,
    ask_ssem,
    ask_rsem,
    cam_ssem,
    cam_rsem,
    cam_sem,
    a2a_ssem,
    a2a_rsem,
    rep_ssem,
    rep_rsem,
    mig_ssem,
    mig_rsem,
    end_ssem,
    end_rsem,
):
    me = lax.axis_index("row")
    rep = lax.axis_index("rep")
    state = (p_s, m_s, v_s)

    def block_rows(ref, b):
        return ref.at[pl.ds(pl.multiple_of(STRIDE * b, 8), P_SIZE), :]

    def lanes_of(ref, b):
        return ref.at[:, pl.ds(pl.multiple_of(BLOCK * b, BLOCK), BLOCK)]

    def load_copy(a, b):
        return pltpu.make_async_copy(
            lanes_of((p_hbm, m_hbm, v_hbm)[a], b), block_rows(state[a], b), local_sem.at[a, b]
        )

    for a in range(3):
        lax.fori_loop(0, nb, lambda b, c: (load_copy(a, b).start(), c)[1], 0)

    barrier = pltpu.get_barrier_semaphore()

    def greet_row(k, c):
        pl.semaphore_signal(barrier, 1, device_id={"row": lax.rem(me + k, nr)}, device_id_type=MESH)
        return c

    def greet_rep(k, c):
        pl.semaphore_signal(barrier, 1, device_id={"rep": lax.rem(rep + k, nx)}, device_id_type=MESH)
        return c

    lax.fori_loop(1, nr, greet_row, 0, unroll=UNROLL)
    lax.fori_loop(1, nx, greet_rep, 0)

    asked_now = jnp.full((nr, BLOCK), -1, jnp.int32)
    lane = lax.broadcasted_iota(jnp.int32, (nr, BLOCK), 1)
    owner_id = lax.broadcasted_iota(jnp.int32, (nr, BLOCK), 0)
    requests = tiles * LISTB
    for i in range(ITERS):
        for s in range(CAP):
            match = (owner_id * CAP + s == request_ref[i : i + 1, :]) & (lane < requests)
            column = jnp.sum(
                jnp.where(match, request_ref[ITERS + i : ITERS + i + 1, :] + 1.0, 0.0), axis=1, keepdims=True
            )
            asked_now = jnp.where(lane == CAP * i + s, column.astype(jnp.int32) - 1, asked_now)
    ask_send[pl.ds(0, nr, stride=8), :] = asked_now
    wide_lane = lax.broadcasted_iota(jnp.int32, (1, BLOCK), 1)
    views = jnp.zeros((1, BLOCK), f32)
    for i in range(ITERS):
        for k in range(11):
            views = jnp.where(wide_lane == 11 * i + k, own_ref[i, 0, k], views)
    cam_recv[pl.ds(pl.multiple_of(8 * rep, 8), 1), :] = views

    pl.semaphore_wait(barrier, nr + nx - 2)

    def row_of(k):
        return lax.rem(me + k, nr), lax.rem(me + nr - k, nr)

    def ask_copy(k, at):
        to, _ = row_of(k)
        return pltpu.make_async_remote_copy(
            src_ref=ask_send.at[pl.ds(pl.multiple_of(8 * to, 8), 1), :],
            dst_ref=ask_recv.at[pl.ds(pl.multiple_of(8 * at, 8), 1), :],
            send_sem=ask_ssem.at[k],
            recv_sem=ask_rsem.at[k],
            device_id={"row": to},
            device_id_type=MESH,
        )

    def cam_copy(k, at):
        return pltpu.make_async_remote_copy(
            src_ref=cam_recv.at[pl.ds(pl.multiple_of(8 * rep, 8), 1), :],
            dst_ref=cam_recv.at[pl.ds(pl.multiple_of(8 * at, 8), 1), :],
            send_sem=cam_ssem.at[k],
            recv_sem=cam_rsem.at[k],
            device_id={"rep": lax.rem(rep + k, nx)},
            device_id_type=MESH,
        )

    lax.fori_loop(1, nr, lambda k, c: (ask_copy(k, me).start(), c)[1], 0)
    for k in range(1, nx):
        cam_copy(k, rep).start()
    own_ask = pl.ds(pl.multiple_of(8 * me, 8), 8)
    ask_recv[own_ask, :] = ask_send[own_ask, :]

    slot_columns = jnp.transpose(
        jnp.concatenate([request_ref[...], jnp.zeros((BLOCK - 8, BLOCK), f32)], axis=0)
    )[0:requests, :]

    square = lax.broadcasted_iota(jnp.int32, (DEPTH, DEPTH), 0), lax.broadcasted_iota(jnp.int32, (DEPTH, DEPTH), 1)
    before = jnp.where(square[0] < square[1], 1.0, 0.0).astype(bf16)
    after = jnp.where(square[0] > square[1], 1.0, 0.0).astype(bf16)
    for part in range(3):
        upper[part * DEPTH : (part + 1) * DEPTH, :] = before
    for part in range(2):
        lower[part * DEPTH : (part + 1) * DEPTH, :] = after
    listed_rows[...] = jnp.zeros_like(listed_rows)
    request_grads[...] = jnp.zeros_like(request_grads)

    for a in range(3):
        lax.fori_loop(0, nb, lambda b, c: (load_copy(a, b).wait(), c)[1], 0)

    def row(ref, r):
        return ref[pl.ds(r, nb, stride=STRIDE), :]

    def put_row(ref, r, x):
        ref[pl.ds(r, nb, stride=STRIDE), :] = x

    def project(i):
        cam = [own_ref[i, 0, k] for k in range(11)]
        affine = [cam[0:3], cam[3:6]]
        rows = functools.partial(row, p_s)
        scales, _, _, rotation = geometry(rows)
        _, conic = conic_of(affine, scales, rotation)
        means = [rows(k) for k in range(3)]
        centre = [
            affine[j][0] * means[0] + affine[j][1] * means[1] + affine[j][2] * means[2] + cam[6 + j] for j in range(2)
        ]
        basis = harmonics(*cam[8:11])
        colours = []
        for k in range(3):
            total = basis[0] * rows(11 + k)
            for j in range(1, 16):
                total = total + basis[j] * rows(11 + 3 * j + k)
            colours.append(0.5 + total)
        return centre + list(conic) + colours + [sigmoid(rows(10))]

    def put_slot(ref, values):
        for c in range(NINE):
            ref[pl.ds(c, nr, stride=PAIR), :] = values[:, c * BLOCK : (c + 1) * BLOCK]

    def get_slot(ref, components=range(NINE)):
        return jnp.concatenate([ref[pl.ds(c, nr, stride=PAIR), :] for c in components], axis=1)

    def nine_rows(p):
        return pl.ds(pl.multiple_of(PAIR * p, 8), NINE)

    def slot_copy(send, recv, which, s, k, at):
        to, _ = row_of(k)
        return pltpu.make_async_remote_copy(
            src_ref=send.at[s, nine_rows(to), :],
            dst_ref=recv.at[s, nine_rows(at), :],
            send_sem=a2a_ssem.at[CAP * which + s, k],
            recv_sem=a2a_rsem.at[CAP * which + s, k],
            device_id={"row": to},
            device_id_type=MESH,
        )

    def slot_start(send, recv, which, s):
        lax.fori_loop(
            1, nr, lambda k, c: (slot_copy(send, recv, which, s, k, me).start(), c)[1], 0, unroll=UNROLL
        )
        recv[s, nine_rows(me), :] = send[s, nine_rows(me), :]

    def slot_arrive(send, recv, which, s):
        lax.fori_loop(
            1,
            nr,
            lambda k, c: (slot_copy(send, recv, which, s, k, row_of(k)[1]).wait_recv(), c)[1],
            0,
            unroll=UNROLL,
        )

    def slot_leave(send, recv, which):
        for s in range(CAP):
            lax.fori_loop(
                1, nr, lambda k, c: (slot_copy(send, recv, which, s, k, me).wait_send(), c)[1], 0, unroll=UNROLL
            )

    def render(i, f_out, f_in, g_out, g_in):
        def list_slot(s):
            slot_lane = CAP * lax.broadcasted_iota(jnp.int32, (requests, nr), 1) + s
            take = jnp.where(slot_columns[:, i : i + 1] == slot_lane.astype(f32), 1.0, 0.0).astype(bf16)
            slot_arrive(f_out, f_in, 2 * i, s)
            pieces = split3(get_slot(f_in.at[s]))
            listed = dot(take, pieces[0]) + dot(take, pieces[1]) + dot(take, pieces[2])
            for c in range(NINE):
                at = pl.ds(c, requests, stride=16)
                fresh = listed[:, BLOCK * c : BLOCK * (c + 1)]
                listed_rows[at, :] = fresh if s == 0 else listed_rows[at, :] + fresh

        def return_slot(s):
            by_request = jnp.concatenate(
                [request_grads[pl.ds(c, requests, stride=16), :] for c in range(NINE)], axis=1
            )
            slot_line = CAP * lax.broadcasted_iota(jnp.int32, (nr, 3 * requests), 0) + s
            back = jnp.where(slot_line.astype(f32) == request_ref[i : i + 1, 0 : 3 * requests], 1.0, 0.0).astype(bf16)
            put_slot(g_out.at[s], dot(back, jnp.concatenate(split3(by_request), axis=0)))
            slot_start(g_out, g_in, 2 * i + 1, s)

        list_slot(0)

        def one_tile(t, carry):
            @pl.when(t == 1)
            def _():
                list_slot(1)

            @pl.when(t == tiles - 1)
            def _():
                return_slot(0)

            for j in range(LISTB):
                listing[:, BLOCK * j : BLOCK * (j + 1)] = listed_rows[
                    pl.ds(pl.multiple_of(16 * (LISTB * t + j), 16), 16), :
                ]
            order = order_ref[i, 0, pl.ds(t, 1), :]
            pick = jnp.where(lax.broadcasted_iota(jnp.int32, (DEPTH, DEPTH), 0) == order, 1.0, 0.0).astype(bf16)
            picks[...] = pick
            parts = dot(jnp.concatenate(split3(listing[...]), axis=0), picks[...])
            splats = parts[0:16] + parts[16:32] + parts[32:48]
            centre_x, centre_y = splats[0:1], splats[1:2]
            conic_a, conic_b, conic_c = splats[2:3], splats[3:4], splats[4:5]
            opacity = splats[8:9]
            ticks = lax.broadcasted_iota(jnp.int32, (SIDE, DEPTH), 0).astype(f32)
            gap_x = (corner_ref[i, 0, t, 0] + ticks + 0.5) - centre_x
            gap_y = (corner_ref[i, 0, t, 1] + ticks + 0.5) - centre_y
            along = -0.5 * conic_a * gap_x * gap_x
            cross = -conic_b * gap_y
            across = -0.5 * conic_c * gap_y * gap_y
            for y in range(SIDE):
                at = slice(SIDE * y, SIDE * (y + 1))
                alpha = opacity * jnp.exp(along + across[y : y + 1] + gap_x * cross[y : y + 1])
                alphas[at, :] = alpha
                for part, piece in enumerate(split3(jnp.log(1.0 - alpha))):
                    logs[at, part * DEPTH : (part + 1) * DEPTH] = piece
            passing[...] = dot(logs[...], upper[...])
            for y in range(SIDE):
                at = slice(SIDE * y, SIDE * (y + 1))
                through = jnp.exp(passing[at, :])
                passing[at, :] = through
                high, low = split2(alphas[at, :] * through)
                weight_high[at, :] = high
                weight_low[at, :] = low
            eight = lax.broadcasted_iota(jnp.int32, (8, 1), 0)
            paint = jnp.where(eight >= 5, splats[0:8], 0.0)
            paint_high = paint.astype(bf16).astype(f32)
            paint_low = paint - paint_high
            both = dot(jnp.concatenate([paint_high, paint_low], axis=0).astype(bf16), weight_high[...], NT)
            high_low = dot(jnp.concatenate([paint_high, paint_high], axis=0).astype(bf16), weight_low[...], NT)
            picture = both[0:8] + both[8:16] + high_low[0:8]
            picture_ref[i, 0, t] = picture[5:8]
            residual = picture - jnp.concatenate([jnp.zeros((5, PIX), f32), target_ref[i, 0, t]], axis=0)
            res_high = residual.astype(bf16).astype(f32)
            res_low = residual - res_high
            pull = dot(
                jnp.transpose(jnp.concatenate([res_high, res_high, res_low, res_low], axis=0)).astype(bf16),
                jnp.concatenate([paint_high, paint_low, paint_high, paint_low], axis=0).astype(bf16),
            )
            pulls[...] = pull
            both = dot(jnp.concatenate([res_high, res_low], axis=0).astype(bf16), weight_high[...])
            high_low = dot(jnp.concatenate([res_high, res_high], axis=0).astype(bf16), weight_low[...])
            colour_grads = both[0:8] + both[8:16] + high_low[0:8]
            for y in range(SIDE):
                at = slice(SIDE * y, SIDE * (y + 1))
                for part, piece in enumerate(split2(alphas[at, :] * passing[at, :] * pulls[at, :])):
                    products[at, part * DEPTH : (part + 1) * DEPTH] = piece
            behind[...] = dot(products[...], lower[...])
            sums = [jnp.zeros((SIDE, DEPTH), f32) for _ in range(3)]
            for y in range(SIDE):
                at = slice(SIDE * y, SIDE * (y + 1))
                alpha = alphas[at, :]
                felt = alpha * (passing[at, :] * pulls[at, :] - behind[at, :] / (1.0 - alpha))
                tall = felt * gap_y[y : y + 1]
                sums = [sums[0] + felt, sums[1] + tall, sums[2] + tall * gap_y[y : y + 1]]

            def over_x(v):
                return jnp.sum(v, axis=0, keepdims=True)

            felt_x = gap_x * sums[0]
            total, total_x, total_xx = over_x(sums[0]), over_x(felt_x), over_x(gap_x * felt_x)
            total_y, total_xy, total_yy = over_x(sums[1]), over_x(gap_x * sums[1]), over_x(sums[2])
            grads = jnp.concatenate(
                [
                    conic_a * total_x + conic_b * total_y,
                    conic_b * total_x + conic_c * total_y,
                    -0.5 * total_xx,
                    -total_xy,
                    -0.5 * total_yy,
                    colour_grads[5:8],
                    total / opacity,
                    jnp.zeros((7, DEPTH), f32),
                ],
                axis=0,
            )
            parts = dot(jnp.concatenate(split3(grads), axis=0), picks[...], NT)
            listed = parts[0:16] + parts[16:32] + parts[32:48]
            for j in range(LISTB):
                request_grads[pl.ds(pl.multiple_of(16 * (LISTB * t + j), 16), 16), :] = listed[
                    :, BLOCK * j : BLOCK * (j + 1)
                ]
            return carry

        lax.fori_loop(0, tiles, one_tile, 0)
        return_slot(1)

    def own_get(a, r):
        return row(state[a], r)

    def own_put(a, r, x):
        put_row(state[a], r, x)

    def step_up(get, put, r, gradient):
        one = 0.9 * get(1, r) + 0.1 * gradient
        two = 0.999 * get(2, r) + 0.001 * gradient * gradient
        put(1, r, one)
        put(2, r, two)
        put(0, r, get(0, r) - learn_rate * one / (jnp.sqrt(two) + adam_epsilon))

    def cameras(i):
        return [[cam_smem[8 * x, 11 * i + k] for k in range(11)] for x in range(nx)]

    def pull_colours(i, get, put, share):
        opacity = sigmoid(get(0, 10))
        fades = share(0, 8)
        for x in range(1, nx):
            fades = fades + share(x, 8)
        step_up(get, put, 10, fades * opacity * (1.0 - opacity))
        bases = [harmonics(*cam[8:11]) for cam in cameras(i)]
        for k in range(3):
            felt = [share(x, 5 + k) for x in range(nx)]
            for j in range(16):
                total = bases[0][j] * felt[0]
                for x in range(1, nx):
                    total = total + bases[x][j] * felt[x]
                step_up(get, put, 11 + 3 * j + k, total)

    def pull_shapes(i, get, put, share):
        scales, quats, inverse, rotation = geometry(lambda r: get(0, r))
        turn = None
        for x, cam in enumerate(cameras(i)):
            affine = [cam[0:3], cam[3:6]]
            spread, (con_a, con_b, con_c) = conic_of(affine, scales, rotation)
            g_a, g_b, g_c = share(x, 2), 0.5 * share(x, 3), share(x, 4)
            left_a, left_b = g_a * con_a + g_b * con_b, g_a * con_b + g_b * con_c
            right_a, right_b = g_b * con_a + g_c * con_b, g_b * con_b + g_c * con_c
            n_xx = -2.0 * (con_a * left_a + con_b * right_a)
            n_xy = -2.0 * (con_a * left_b + con_b * right_b)
            n_yy = -2.0 * (con_b * left_b + con_c * right_b)
            felt = [
                [n_xx * spread[0][k] + n_xy * spread[1][k] for k in range(3)],
                [n_xy * spread[0][k] + n_yy * spread[1][k] for k in range(3)],
            ]
            stretch = [felt[0][k] * spread[0][k] + felt[1][k] * spread[1][k] for k in range(3)]
            twist = [
                [(affine[0][j] * felt[0][k] + affine[1][j] * felt[1][k]) * scales[k] for k in range(3)]
                for j in range(3)
            ]
            moved = [affine[0][j] * share(x, 0) + affine[1][j] * share(x, 1) for j in range(3)]
            if turn is None:
                stretches, turn, moves = stretch, twist, moved
            else:
                stretches = [u + v for u, v in zip(stretches, stretch)]
                turn = [[u + v for u, v in zip(a, b)] for a, b in zip(turn, twist)]
                moves = [u + v for u, v in zip(moves, moved)]
        w, x, y, z = quats
        d = turn
        unit = [
            2.0 * (z * (d[1][0] - d[0][1]) + y * (d[0][2] - d[2][0]) + x * (d[2][1] - d[1][2])),
            2.0
            * (
                y * (d[0][1] + d[1][0])
                + z * (d[0][2] + d[2][0])
                + w * (d[2][1] - d[1][2])
                - 2.0 * x * (d[1][1] + d[2][2])
            ),
            2.0
            * (
                x * (d[0][1] + d[1][0])
                + w * (d[0][2] - d[2][0])
                + z * (d[1][2] + d[2][1])
                - 2.0 * y * (d[0][0] + d[2][2])
            ),
            2.0
            * (
                w * (d[1][0] - d[0][1])
                + x * (d[0][2] + d[2][0])
                + y * (d[1][2] + d[2][1])
                - 2.0 * z * (d[0][0] + d[1][1])
            ),
        ]
        inner = unit[0] * w + unit[1] * x + unit[2] * y + unit[3] * z
        for k in range(3):
            step_up(get, put, k, moves[k])
        for k in range(3):
            step_up(get, put, 3 + k, stretches[k])
        for k in range(4):
            step_up(get, put, 6 + k, (unit[k] - quats[k] * inner) * inverse)

    parts_of = ((5, 4), (0, 5))

    def share_copy(i, part, k, at):
        first, count = parts_of[part]

        def rows_at(x):
            return pl.ds(pl.multiple_of((NINE * x + first) * nb, 8), count * nb)

        return pltpu.make_async_remote_copy(
            src_ref=shared.at[i, rows_at(rep), :],
            dst_ref=shared.at[i, rows_at(at), :],
            send_sem=rep_ssem.at[2 * i + part, k],
            recv_sem=rep_rsem.at[2 * i + part, k],
            device_id={"rep": lax.rem(rep + k, nx)},
            device_id_type=MESH,
        )

    hand = MIGH * 3 * STRIDE
    round_rows = MIGH * ROUND

    def neighbour(side):
        return {"row": lax.rem(me + (nr - 1 if side == 0 else 1), nr)}

    def hand_copy(side):
        return pltpu.make_async_remote_copy(
            src_ref=mig_send.at[pl.ds(side * hand, hand), :],
            dst_ref=mig_recv.at[pl.ds((1 - side) * hand, hand), :],
            send_sem=mig_ssem.at[side],
            recv_sem=mig_rsem.at[side],
            device_id=neighbour(side),
            device_id_type=MESH,
        )

    def end_copy(side):
        return pltpu.make_async_remote_copy(
            src_ref=end_send.at[pl.ds(side * round_rows, round_rows), :],
            dst_ref=end_recv.at[pl.ds((1 - side) * round_rows, round_rows), :],
            send_sem=end_ssem.at[side],
            recv_sem=end_rsem.at[side],
            device_id=neighbour(side),
            device_id_type=MESH,
        )

    def hand_over():
        for side in range(2):
            for j in range(MIGH):
                leaving = jnp.full((STRIDE, BLOCK), migration_ref[0, side, j], jnp.int32)
                for a in range(3):
                    at = side * hand + (3 * j + a) * STRIDE
                    chosen = state[a][0:STRIDE, :]
                    for b in range(1, nb):
                        chosen = jnp.where(leaving == b, state[a][STRIDE * b : STRIDE * (b + 1), :], chosen)
                    mig_send[at : at + STRIDE, :] = chosen
            hand_copy(side).start()

    def hand_gradients(share):
        count = 2 * MIGH
        line = lax.broadcasted_iota(jnp.int32, (8, 3 * nb), 0)
        block_lane = lax.rem(lax.broadcasted_iota(jnp.int32, (8, 3 * nb), 1), nb)
        mine = jnp.full((8, 3 * nb), -1, jnp.int32)
        for side in range(2):
            for j in range(MIGH):
                mine = jnp.where(line == MIGH * side + j, migration_ref[0, side, j], mine)
        choose = jnp.where(mine == block_lane, 1.0, 0.0)
        choose = jnp.concatenate([choose, jnp.zeros_like(choose)], axis=0).astype(bf16)
        for x in range(nx):
            values = jnp.concatenate([share(x, c) for c in range(NINE)], axis=1)
            chosen = dot(choose, jnp.concatenate(split3(values), axis=0))
            for c in range(NINE):
                end_send[pl.ds(NINE * x + c, count, stride=ROUND), :] = chosen[0:count, BLOCK * c : BLOCK * (c + 1)]
        for side in range(2):
            end_copy(side).start()

    asked_columns = asked_lines = None
    for i in range(ITERS):
        projected = jnp.concatenate(project(i), axis=1)
        if i == 0:

            def asked(k, c):
                copy = ask_copy(k, row_of(k)[1])
                copy.wait_recv()
                copy.wait_send()
                return c

            lax.fori_loop(1, nr, asked, 0)
            asked_all = ask_recv[pl.ds(0, nr, stride=8), :].astype(f32)
            asked_columns = asked_all
            asked_lines = jnp.transpose(
                asked_all
                if nr == BLOCK
                else jnp.concatenate([asked_all, jnp.zeros((BLOCK - nr, BLOCK), f32)], axis=0)
            )
        block_lane = lax.rem(lax.broadcasted_iota(jnp.int32, (nr, 3 * nb), 1), nb).astype(f32)
        serve = jnp.concatenate(
            [
                jnp.where(asked_columns[:, CAP * i + s : CAP * i + s + 1] == block_lane, 1.0, 0.0)
                for s in range(CAP)
            ],
            axis=0,
        ).astype(bf16)
        slots = jnp.concatenate(split3(projected), axis=0)
        for s in range(CAP):
            put_slot(f_send.at[i, s], dot(serve[s * nr : (s + 1) * nr], slots))
            slot_start(f_send.at[i], f_recv.at[i], 2 * i, s)
        render(i, f_send.at[i], f_recv.at[i], g_send.at[i], g_recv.at[i])
        slot_leave(f_send.at[i], f_recv.at[i], 2 * i)
        block_line = lax.broadcasted_iota(jnp.int32, (nb, nr), 0).astype(f32)
        gathers = [
            jnp.where(block_line == asked_lines[CAP * i + s : CAP * i + s + 1, 0:nr], 1.0, 0.0).astype(bf16)
            for s in range(CAP)
        ]

        def sum_slot(s, first, count):
            pieces = split3(get_slot(g_recv.at[i, s], range(first, first + count)))
            return dot(gathers[s], pieces[0]) + dot(gathers[s], pieces[1]) + dot(gathers[s], pieces[2])

        slot_arrive(g_send.at[i], g_recv.at[i], 2 * i + 1, 0)
        sums = [sum_slot(0, *parts_of[part]) for part in range(2)]
        slot_arrive(g_send.at[i], g_recv.at[i], 2 * i + 1, 1)
        for part in range(2):
            first, count = parts_of[part]
            summed = sums[part] + sum_slot(1, first, count)
            for c in range(count):
                shared[i, pl.ds(pl.multiple_of((NINE * rep + first + c) * nb, 8), nb), :] = summed[
                    :, BLOCK * c : BLOCK * (c + 1)
                ]
            for k in range(1, nx):
                share_copy(i, part, k, rep).start()
        slot_leave(g_send.at[i], g_recv.at[i], 2 * i + 1)
        if i == 0:
            for k in range(1, nx):
                copy = cam_copy(k, lax.rem(rep + nx - k, nx))
                copy.wait_recv()
                copy.wait_send()
            table = pltpu.make_async_copy(cam_recv, cam_smem, cam_sem)
            table.start()
            table.wait()

        def own_share(x, c):
            at = (x * NINE + c) * nb
            return shared[i, at : at + nb, :]

        def arrive_share(part):
            for k in range(1, nx):
                copy = share_copy(i, part, k, lax.rem(rep + nx - k, nx))
                copy.wait_recv()
                copy.wait_send()

        arrive_share(0)
        pull_colours(i, own_get, own_put, own_share)
        arrive_share(1)
        if i == ITERS - 1:
            hand_gradients(own_share)
        pull_shapes(i, own_get, own_put, own_share)
        if i == ITERS - 2:
            hand_over()

    for side in range(2):
        hand_copy(side).wait_recv()
        hand_copy(side).wait_send()
        end_copy(side).wait_recv()
        end_copy(side).wait_send()

    def come_get(a, r):
        return mig_recv[pl.ds(a * STRIDE + r, 2 * MIGH, stride=3 * STRIDE), :]

    def come_put(a, r, x):
        mig_recv[pl.ds(a * STRIDE + r, 2 * MIGH, stride=3 * STRIDE), :] = x

    def come_share(x, c):
        return end_recv[pl.ds(NINE * x + c, 2 * MIGH, stride=ROUND), :]

    pull_colours(ITERS - 1, come_get, come_put, come_share)
    pull_shapes(ITERS - 1, come_get, come_put, come_share)

    def settle(b, carry):
        for a in range(3):
            at = pl.ds(pl.multiple_of(STRIDE * b, STRIDE), STRIDE)
            block = state[a][at, :]
            for side in range(2):
                for j in range(MIGH):
                    source = side * hand + (3 * j + a) * STRIDE
                    here = jnp.full((STRIDE, BLOCK), migration_ref[0, side, j], jnp.int32) == b
                    block = jnp.where(here, mig_recv[source : source + STRIDE, :], block)
            state[a][at, :] = block
            store_copy(a, b).start()
        return carry

    def store_copy(a, b):
        return pltpu.make_async_copy(
            block_rows(state[a], b), lanes_of((p_out, m_out, v_out)[a], b), out_sem.at[a, b]
        )

    lax.fori_loop(0, nb, settle, 0)
    for a in range(3):
        lax.fori_loop(0, nb, lambda b, c: (store_copy(a, b).wait(), c)[1], 0)


def local(
    params,
    first_moment,
    second_moment,
    camera,
    tile_corner,
    tile_owner,
    tile_block,
    depth_order,
    targets,
    migration,
):
    nr, nx = lax.axis_size("row"), lax.axis_size("rep")
    local_gauss = params.shape[1]
    nb = local_gauss // BLOCK
    tiles = tile_owner.shape[2]
    requests = tiles * LISTB
    owner = tile_owner.reshape(ITERS, requests)
    block = tile_block.reshape(ITERS, requests)
    position = jnp.arange(requests, dtype=jnp.int32)
    same = (owner[:, :, None] == owner[:, None, :]) & (position[None, :] < position[:, None])
    later = jnp.any(same, axis=2) | (position >= requests - LISTB)[None, :]
    slot = owner * CAP + later.astype(jnp.int32)
    wide = jnp.concatenate([slot, slot, slot], axis=1).astype(f32)
    table = jnp.concatenate(
        [
            jnp.pad(wide, ((0, 0), (0, BLOCK - 3 * requests)), constant_values=-1.0),
            jnp.pad(block.astype(f32), ((0, 0), (0, BLOCK - requests))),
            jnp.zeros((8 - 2 * ITERS, BLOCK), f32),
        ],
        axis=0,
    )

    vmem = pl.BlockSpec(memory_space=pltpu.VMEM)
    smem = pl.BlockSpec(memory_space=pltpu.SMEM)
    hbm = pl.BlockSpec(memory_space=pl.ANY)
    size = jax.ShapeDtypeStruct((P_SIZE, local_gauss), f32)
    dma = pltpu.SemaphoreType.DMA
    new_params, new_first, new_second, pictures = pl.pallas_call(
        functools.partial(kernel, nr, nx, nb, tiles),
        out_shape=(size, size, size, jax.ShapeDtypeStruct((ITERS, 1, tiles, 3, PIX), f32)),
        in_specs=[smem] * 3 + [vmem] * 3 + [hbm] * 3,
        out_specs=(hbm, hbm, hbm, vmem),
        scratch_shapes=[
            pltpu.VMEM((STRIDE * nb, BLOCK), f32),
            pltpu.VMEM((STRIDE * nb, BLOCK), f32),
            pltpu.VMEM((STRIDE * nb, BLOCK), f32),
            pltpu.VMEM((8 * nr, BLOCK), jnp.int32),
            pltpu.VMEM((8 * nr, BLOCK), jnp.int32),
            pltpu.VMEM((8 * nx, BLOCK), f32),
            pltpu.SMEM((8 * nx, BLOCK), f32),
            pltpu.VMEM((ITERS, CAP, PAIR * nr, BLOCK), f32),
            pltpu.VMEM((ITERS, CAP, PAIR * nr, BLOCK), f32),
            pltpu.VMEM((ITERS, CAP, PAIR * nr, BLOCK), f32),
            pltpu.VMEM((ITERS, CAP, PAIR * nr, BLOCK), f32),
            pltpu.VMEM((ITERS, nx * NINE * nb, BLOCK), f32),
            pltpu.VMEM((2 * MIGH * 3 * STRIDE, BLOCK), f32),
            pltpu.VMEM((2 * MIGH * 3 * STRIDE, BLOCK), f32),
            pltpu.VMEM((2 * MIGH * ROUND, BLOCK), f32),
            pltpu.VMEM((2 * MIGH * ROUND, BLOCK), f32),
            pltpu.VMEM((16, DEPTH), f32),
            pltpu.VMEM((16 * requests, BLOCK), f32),
            pltpu.VMEM((DEPTH, DEPTH), bf16),
            pltpu.VMEM((3 * DEPTH, DEPTH), bf16),
            pltpu.VMEM((2 * DEPTH, DEPTH), bf16),
            pltpu.VMEM((PIX, 3 * DEPTH), bf16),
            pltpu.VMEM((PIX, DEPTH), f32),
            pltpu.VMEM((PIX, DEPTH), f32),
            pltpu.VMEM((PIX, DEPTH), bf16),
            pltpu.VMEM((PIX, DEPTH), bf16),
            pltpu.VMEM((PIX, DEPTH), f32),
            pltpu.VMEM((PIX, 2 * DEPTH), bf16),
            pltpu.VMEM((PIX, DEPTH), f32),
            pltpu.VMEM((16 * requests, BLOCK), f32),
            dma((3, nb)),
            dma((3, nb)),
            dma((nr,)),
            dma((nr,)),
            dma((nx,)),
            dma((nx,)),
            dma(()),
            dma((2 * ITERS * CAP, nr)),
            dma((2 * ITERS * CAP, nr)),
            dma((2 * ITERS, nx)),
            dma((2 * ITERS, nx)),
            dma((2,)),
            dma((2,)),
            dma((2,)),
            dma((2,)),
        ],
        compiler_params=pltpu.CompilerParams(
            collective_id=0, has_side_effects=True, vmem_limit_bytes=48 * 1024 * 1024
        ),
        cost_estimate=pl.CostEstimate(flops=20_000_000_000, bytes_accessed=6_000_000, transcendentals=4_000_000),
        name="train",
    )(
        tile_corner,
        camera,
        migration,
        table,
        depth_order,
        targets,
        params,
        first_moment,
        second_moment,
    )
    return new_params, new_first, new_second, pictures


def solution(mesh):
    return jax.shard_map(
        local,
        mesh=mesh,
        in_specs=(
            P(None, "row"),
            P(None, "row"),
            P(None, "row"),
            P(None, "rep", None),
            P(None, "rep", "row", None),
            P(None, "rep", "row", None),
            P(None, "rep", "row", None),
            P(None, "rep", "row", None),
            P(None, "rep", "row", None, None),
            P("row", None, None),
        ),
        out_specs=(
            P(None, "row"),
            P(None, "row"),
            P(None, "row"),
            P(None, "rep", "row", None, None),
        ),
        check_vma=False,
    )
```
